128 devices in a mesh: ctx: 64 (over x, z, y), tp: 2 (over core).
Axes of the slice: x: 4, y: 4, z: 4, core: 2. Of those that a mesh axis runs over, the one named last changes fastest.
Arguments:
- inputs: bfloat16 [32768, 4, 1024], P('ctx', None, 'tp'), may hold values from -6 to 6
- grad_out: bfloat16 [32768, 4, 1024], P('ctx', None, 'tp'), may hold values from -6 to 6
- dt_raw: float32 [4, 16, 32768], P(None, 'tp', 'ctx'), may hold values from -14 to 0
- dt_bias: float32 [4, 16], P(None, 'tp'), may hold values from -0.5 to 0.5
- a_log: float32 [4, 16], P(None, 'tp'), may hold values from -0.5 to 0.5
- b_proj: bfloat16 [32768, 4, 64], P('ctx'), may hold values from -2 to 2
- c_proj: bfloat16 [32768, 4, 64], P('ctx'), may hold values from -2 to 2
Outputs:
- grad_inputs: bfloat16 [32768, 4, 1024], P('ctx', None, 'tp')
- grad_raw: float32 [4, 16, 32768], P(None, 'tp', 'ctx')
- grad_alog: float32 [4, 16], P(None, 'tp')
- grad_bias: float32 [4, 16], P(None, 'tp')
- grad_b: bfloat16 [32768, 4, 64], P('ctx', 'tp')
- grad_c: bfloat16 [32768, 4, 64], P('ctx', 'tp')
The draws below stay inside these ranges and needn't reach their ends.
All inputs are finite; a program needn't handle non-finite values.
Results may differ from the reference program's by a relative error of at most 0.011.
Values may be sent and summed in bfloat16 or wider, within the bound.
A program may use at most 448 MiB of HBM per device.

```python
import math
import jax
import jax.numpy as jnp
from jax import lax

HEAD_DIM = 64
STATE = 64
SHARED_GROUPS = 4
TOK_DEV = 512
HEADS_PER_GROUP = 16
SEQUENCE_TOKENS = 32768


def draw_dt_raw(key, part):
    key = jax.random.fold_in(key, 7)
    random_keys = jax.random.split(key, 6)
    blocks = SEQUENCE_TOKENS // TOK_DEV
    shape = (SHARED_GROUPS, HEADS_PER_GROUP, 1, 1)
    picked = jax.random.randint(random_keys[4], shape, 0, 8) == 0
    quick = jnp.exp(jax.random.uniform(random_keys[5], shape, jnp.float32, math.log(0.02), math.log(0.04)))
    slow = jnp.exp(jax.random.uniform(random_keys[0], shape, jnp.float32, math.log(5e-05), math.log(0.001)))
    first_head_index = jnp.where(picked, quick, slow)
    block_multiplier = jnp.exp(jax.random.uniform(random_keys[1], (SHARED_GROUPS, HEADS_PER_GROUP, blocks, 1), jnp.float32, math.log(0.5), math.log(2.0)))
    token_multiplier = jax.random.uniform(random_keys[2], (SHARED_GROUPS, HEADS_PER_GROUP, blocks, TOK_DEV), jnp.float32, 0.5, 1.5)
    segment_offsets = jax.random.randint(random_keys[3], (SHARED_GROUPS, HEADS_PER_GROUP, 3, 1), 0, SEQUENCE_TOKENS)
    token_positions = jnp.arange(SEQUENCE_TOKENS)[None, None, None, :]
    segments = jnp.any(segment_offsets == token_positions, axis=2).astype(jnp.float32)
    time_step_width = (first_head_index * block_multiplier * token_multiplier).reshape(SHARED_GROUPS, HEADS_PER_GROUP, SEQUENCE_TOKENS) + 0.4 * segments
    return jnp.log(jnp.expm1(time_step_width))


def steps_of(stream_key, shape, cuts, smallest, high):
    gain = 1.0
    for dim, blocks in cuts:
        draws = jax.random.uniform(jax.random.fold_in(jax.random.fold_in(stream_key, 6), dim), (blocks,), jnp.float32, smallest / len(cuts), high / len(cuts))
        gain = gain * jnp.repeat(jnp.exp(draws), shape[dim] // blocks).reshape((-1,) + (1,) * (len(shape) - 1 - dim))
    return gain


def bell_draw(stream_key, extent, scale, limit, cuts=(), kind=jnp.bfloat16):
    gain = steps_of(stream_key, extent, cuts, -0.22, 0.18) if cuts else 1.0
    array = jax.random.normal(stream_key, extent, jnp.float32) * scale * gain
    return jnp.minimum(jnp.maximum(array, -limit), limit).astype(kind)


def setup_inputs(seed: int = 0) -> dict:
    keys = jax.random.split(jax.random.key(seed), 8)
    return {
        "inputs": bell_draw(keys[0], (SEQUENCE_TOKENS, SHARED_GROUPS, HEADS_PER_GROUP * HEAD_DIM), 1.0, 6.0, ((0, 64), (2, 2))),
        "grad_out": bell_draw(keys[1], (SEQUENCE_TOKENS, SHARED_GROUPS, HEADS_PER_GROUP * HEAD_DIM), 1.0, 6.0, ((0, 64), (2, 2))),
        "dt_raw": draw_dt_raw(jax.random.fold_in(keys[7], 71), 0),
        "dt_bias": jnp.clip(jax.random.uniform(keys[3], (SHARED_GROUPS, HEADS_PER_GROUP), jnp.float32, -0.5, 0.5) * steps_of(keys[3], (SHARED_GROUPS, HEADS_PER_GROUP), ((1, 2),), -0.4, 0.0), -0.5, 0.5),
        "a_log": jnp.clip(jax.random.uniform(keys[4], (SHARED_GROUPS, HEADS_PER_GROUP), jnp.float32, -0.5, 0.5) * steps_of(keys[4], (SHARED_GROUPS, HEADS_PER_GROUP), ((1, 2),), -0.4, 0.0), -0.5, 0.5),
        "b_proj": bell_draw(keys[5], (SEQUENCE_TOKENS, SHARED_GROUPS, STATE), 0.25, 2.0, ((0, 64),)),
        "c_proj": bell_draw(keys[6], (SEQUENCE_TOKENS, SHARED_GROUPS, STATE), 0.25, 2.0, ((0, 64),)),
    }


HIGHEST = lax.Precision.HIGHEST


def decays_of(raw_rates, dt_bias, a_log):
    time_step_width = jax.nn.softplus(raw_rates + dt_bias[:, :, None])
    rates = jnp.exp(a_log)
    log_decay = -time_step_width * rates[:, :, None]
    cumulative = jnp.cumsum(log_decay, axis=2)
    return time_step_width, rates, cumulative


def weighted(inputs4, grad4, time_step_width, cumulative):
    final = cumulative[:, :, -1:]
    end_weight = jnp.exp(final - cumulative) * time_step_width
    start_weight = jnp.exp(cumulative)
    scaled_input = (inputs4 * jnp.transpose(end_weight, (2, 0, 1))[..., None]).astype(jnp.bfloat16)
    scaled_grad = (grad4 * jnp.transpose(start_weight, (2, 0, 1))[..., None]).astype(jnp.bfloat16)
    return scaled_input, scaled_grad, start_weight


def split_heads(inputs, grad_out, raw_rates):
    length, groups, width = inputs.shape
    heads = raw_rates.shape[1]
    inputs4 = inputs.reshape(length, groups, heads, width // heads)
    grad4 = grad_out.reshape(length, groups, heads, width // heads)
    return inputs4, grad4


def summaries(inputs, grad_out, raw_rates, b_blk, c_blk, dt_bias, a_log):
    inputs4, grad4 = split_heads(inputs, grad_out, raw_rates)
    time_step_width, rates, cumulative = decays_of(raw_rates, dt_bias, a_log)
    scaled_input, scaled_grad, start_weight = weighted(inputs4, grad4, time_step_width, cumulative)
    ends = jnp.einsum("lghp,lgn->ghpn", scaled_input.astype(jnp.float32), b_blk.astype(jnp.float32), precision=HIGHEST)
    starts = jnp.einsum("lghp,lgn->ghpn", scaled_grad.astype(jnp.float32), c_blk.astype(jnp.float32), precision=HIGHEST)
    return jnp.exp(cumulative[:, :, -1]), ends, starts


def within_block(inputs_g, grad_g, b_g, c_g, cumulative, time_step_width):
    length = inputs_g.shape[0]
    order = jnp.arange(length)
    lower = order[:, None] >= order[None, :]
    intersection = jnp.dot(c_g, b_g.T, preferred_element_type=jnp.float32)
    spread = jnp.where(lower, cumulative[:, :, None] - cumulative[:, None, :], 0.0)
    decay_mat = jnp.where(lower, jnp.exp(spread), 0.0)
    pair = jnp.einsum("lhp,mhp->hlm", grad_g.astype(jnp.float32), inputs_g.astype(jnp.float32))
    mixing = (decay_mat * intersection).astype(jnp.bfloat16)
    grad_state = jnp.einsum("hlm,lhp->mhp", mixing.astype(jnp.float32), grad_g.astype(jnp.float32))
    weights = decay_mat * pair * time_step_width[:, None, :]
    weights_low = weights.astype(jnp.bfloat16).astype(jnp.float32)
    grad_c = jnp.einsum("hlm,mn->ln", weights_low, b_g.astype(jnp.float32))
    grad_b = jnp.einsum("hlm,ln->mn", weights_low, c_g.astype(jnp.float32))
    terms = weights * intersection
    balance = jnp.sum(terms, axis=2) - jnp.sum(terms, axis=1)
    return grad_state, grad_b, grad_c, balance


def block_out(inputs, grad_out, raw_rates, b_blk, c_blk, states_in, grads_in, dt_bias, a_log):
    length, groups, width = inputs.shape
    inputs4, grad4 = split_heads(inputs, grad_out, raw_rates)
    time_step_width, rates, cumulative = decays_of(raw_rates, dt_bias, a_log)
    scaled_input, scaled_grad, start_weight = weighted(inputs4, grad4, time_step_width, cumulative)
    final = cumulative[:, :, -1]
    state_low = states_in.astype(jnp.bfloat16).astype(jnp.float32)
    grad_low = grads_in.astype(jnp.bfloat16).astype(jnp.float32)
    tail_weight = jnp.transpose(jnp.exp(final[:, :, None] - cumulative), (2, 0, 1))[..., None]
    cross_grad = jnp.einsum("lgn,ghpn->lghp", b_blk.astype(jnp.float32), grad_low) * tail_weight
    cross_out = jnp.einsum("lgn,ghpn->lghp", c_blk.astype(jnp.float32), state_low) * jnp.transpose(start_weight, (2, 0, 1))[..., None]
    cross_b = jnp.einsum("lghp,ghpn->lgn", scaled_input.astype(jnp.float32), grad_low)
    cross_c = jnp.einsum("lghp,ghpn->lgn", scaled_grad.astype(jnp.float32), state_low)
    parts = lax.map(lambda item: within_block(*item), (jnp.moveaxis(inputs4, 1, 0), jnp.moveaxis(grad4, 1, 0), jnp.moveaxis(b_blk, 1, 0), jnp.moveaxis(c_blk, 1, 0), cumulative, time_step_width))
    grad_state = jnp.moveaxis(parts[0], 0, 1) + cross_grad
    step_rows = jnp.transpose(time_step_width, (2, 0, 1))
    grad_inputs = (step_rows[..., None] * grad_state).astype(jnp.bfloat16).reshape(length, groups, width)
    along = jnp.transpose(jnp.sum(inputs4 * grad_state, axis=3), (1, 2, 0))
    inflow = jnp.transpose(jnp.sum(grad4 * cross_out, axis=3), (1, 2, 0))
    outflow = time_step_width * jnp.transpose(jnp.sum(inputs4 * cross_grad, axis=3), (1, 2, 0))
    through = jnp.exp(final) * jnp.sum(grads_in * states_in, axis=(2, 3))
    balance = parts[3] + inflow - outflow
    log_grad = jnp.flip(jnp.cumsum(jnp.flip(balance, 2), axis=2), 2) + jnp.sum(outflow, axis=2, keepdims=True) + through[:, :, None]
    grad_step = along - rates[:, :, None] * log_grad
    grad_raw = grad_step * jax.nn.sigmoid(raw_rates + dt_bias[:, :, None])
    grad_alog = jnp.sum(log_grad * (-time_step_width * rates[:, :, None]), axis=2)
    grad_bias = jnp.sum(grad_raw, axis=2)
    grad_b = jnp.moveaxis(parts[1], 0, 1) + cross_b
    grad_c = jnp.moveaxis(parts[2], 0, 1) + cross_c
    return grad_inputs, grad_raw, grad_alog, grad_bias, grad_b, grad_c


def reference(inputs, grad_out, dt_raw, dt_bias, a_log, b_proj, c_proj):
    blocks = SEQUENCE_TOKENS // TOK_DEV
    in_blk = inputs.reshape(blocks, TOK_DEV, SHARED_GROUPS, HEADS_PER_GROUP * HEAD_DIM)
    grad_blk = grad_out.reshape(blocks, TOK_DEV, SHARED_GROUPS, HEADS_PER_GROUP * HEAD_DIM)
    raw_blk = jnp.transpose(dt_raw.reshape(SHARED_GROUPS, HEADS_PER_GROUP, blocks, TOK_DEV), (2, 0, 1, 3))
    b_blk = b_proj.reshape(blocks, TOK_DEV, SHARED_GROUPS, STATE)
    c_blk = c_proj.reshape(blocks, TOK_DEV, SHARED_GROUPS, STATE)

    def first_pass(item):
        return summaries(*item, dt_bias, a_log)

    decays, ends, starts = lax.map(first_pass, (in_blk, grad_blk, raw_blk, b_blk, c_blk))

    def carry_step(carry, item):
        decay, local = item
        return decay[:, :, None, None] * carry + local, carry

    zero = jnp.zeros((SHARED_GROUPS, HEADS_PER_GROUP, HEAD_DIM, STATE), jnp.float32)
    _, states_in = lax.scan(carry_step, zero, (decays, ends))
    _, grads_in = lax.scan(carry_step, zero, (decays, starts), reverse=True)

    def second_pass(item):
        return block_out(*item, dt_bias, a_log)

    outs = lax.map(second_pass, (in_blk, grad_blk, raw_blk, b_blk, c_blk, states_in, grads_in))
    grad_inputs = outs[0].reshape(SEQUENCE_TOKENS, SHARED_GROUPS, HEADS_PER_GROUP * HEAD_DIM)
    grad_raw = jnp.transpose(outs[1], (1, 2, 0, 3)).reshape(SHARED_GROUPS, HEADS_PER_GROUP, SEQUENCE_TOKENS)
    grad_alog = jnp.sum(outs[2], axis=0)
    grad_bias = jnp.sum(outs[3], axis=0)
    grad_b = outs[4].reshape(SEQUENCE_TOKENS, SHARED_GROUPS, STATE).astype(jnp.bfloat16)
    grad_c = outs[5].reshape(SEQUENCE_TOKENS, SHARED_GROUPS, STATE).astype(jnp.bfloat16)
    return (grad_inputs, grad_raw, grad_alog, grad_bias, grad_b, grad_c)
```

```python
import functools

import jax
import jax.numpy as jnp
from jax import lax
from jax.experimental import pallas as pl
from jax.experimental.pallas import tpu as pltpu
from jax.sharding import PartitionSpec as P

HIGHEST = lax.Precision.HIGHEST
F32 = jnp.float32
BF16 = jnp.bfloat16
MESH = pl.DeviceIdType.MESH

TOK = 512
GROUPS = 4
HEADS = 8
DIM = 64
CHUNK = 64
CHUNKS = TOK // CHUNK
PAIRS = CHUNKS // 2
ROWS = CHUNK * GROUPS
WIDE = HEADS * DIM
GH = GROUPS * HEADS
TILES = 64


def iota(shape, axis):
    return lax.broadcasted_iota(jnp.int32, shape, axis)


def ones(condition, kind=F32):
    return jnp.where(condition, 1.0, 0.0).astype(kind)


def dot(a, b, contract=((1,), (0,)), precision=None):
    return lax.dot_general(a, b, (contract, ((), ())), preferred_element_type=F32, precision=precision)


NT = ((1,), (1,))
TN = ((0,), (0,))


def kernel(
    n, x_ref, g_ref, dt_ref, bias_ref, alog_ref, bt_ref, ct_ref,
    gin_ref, graw_ref, galog_ref, gbias_ref, gb_ref, gc_ref,
    st_ref, sx_ref, xt_ref, gt_ref, bzt_ref, czt_ref, bz_ref, cz_ref, e_ref, f_ref, mul_ref,
    s_ref, g2_ref, sp_ref, gp_ref, z_ref, q_ref, gbacc_ref, gcacc_ref, th_ref,
    r2_ref, r2t_ref, gmask_ref, low_ref, wmask_ref,
    decsrc_ref, decall_ref, decx_ref, snd1_ref, rcv1_ref, snd2_ref, rcv2_ref,
    tsnd_ref, trcv_ref, tail_ref, tailall_ref,
    ss0, rs0, ss1, rs1, ss2, rs2, ss3, rs3, st4, rt4,
):
    m = TILES // n
    me = lax.axis_index("ctx")
    core = lax.axis_index("tp")
    other = 1 - core

    barrier = pltpu.get_barrier_semaphore()

    def greet(i, _):
        pl.semaphore_signal(barrier, inc=1, device_id=(lax.rem(me + i, n), core), device_id_type=MESH)
        return 0

    lax.fori_loop(1, n, greet, 0)
    pl.semaphore_signal(barrier, inc=1, device_id=(me, other), device_id_type=MESH)

    def to_peer(src, dst, ssem, rsem, i):
        peer = lax.rem(me + i, n)
        return pltpu.make_async_remote_copy(
            src_ref=src(peer), dst_ref=dst.at[me], send_sem=ssem.at[i], recv_sem=rsem.at[i],
            device_id=(peer, core), device_id_type=MESH,
        )

    def each_peer(action):
        def lap(i, _):
            action(i)
            return 0

        lax.fori_loop(1, n, lap, 0)

    diag = iota((HEADS, HEADS), 0) == iota((HEADS, HEADS), 1)

    def column(ref):
        return jnp.concatenate(
            [jnp.sum(jnp.where(diag, ref[g : g + 1, :], 0.0), axis=1, keepdims=True) for g in range(GROUPS)], axis=0
        )

    rates = jnp.exp(column(alog_ref))
    u = dt_ref[...] + column(bias_ref)
    step = jnp.maximum(u, 0.0) + jnp.log1p(jnp.exp(-jnp.abs(u)))
    ld = -step * rates
    sq0, sq1 = iota((128, 128), 0), iota((128, 128), 1)
    same = sq0 // CHUNK == sq1 // CHUNK
    tri = ones(same & (sq0 <= sq1))
    block = ones(same)

    def along_tokens(value, table):
        return jnp.concatenate(
            [dot(value[:, 128 * j : 128 * j + 128], table, precision=HIGHEST) for j in range(TOK // 128)], axis=1
        )

    cum = along_tokens(ld, tri)
    half = along_tokens(ld, block) * 0.5
    sg = jnp.exp(cum - half)
    sx = step * jnp.exp(half - cum)
    sg_hi = sg.astype(BF16).astype(F32)
    sx_hi = sx.astype(BF16).astype(F32)
    stack = jnp.concatenate([sg_hi, sg - sg_hi, sx_hi, sx - sx_hi], axis=0)
    for j in range(TOK // 128):
        st_ref[128 * j : 128 * j + 128, :] = stack[:, 128 * j : 128 * j + 128].T.astype(BF16)

    total = jnp.sum(ld, axis=1, keepdims=True)
    row = jnp.sum(jnp.where(iota((GH, 128), 0) == iota((GH, 128), 1), total, 0.0), axis=0, keepdims=True)
    decsrc_ref[...] = jnp.broadcast_to(row, (8, 128))
    decall_ref[me] = decsrc_ref[...]
    pl.semaphore_wait(barrier, n)
    dec_copy = functools.partial(to_peer, lambda peer: decsrc_ref, decall_ref, ss0, rs0)
    each_peer(lambda i: dec_copy(i).start())

    first = ones(iota((TOK, CHUNKS * GROUPS), 0) == (iota((TOK, CHUNKS * GROUPS), 1) // GROUPS) * CHUNK)
    half8 = dot(half, first, precision=HIGHEST)
    half8 = jnp.where(iota((GH, 32), 0) // HEADS == iota((GH, 32), 1) % GROUPS, half8, 0.0)
    by_head = ones(iota((GH, WIDE), 0) % HEADS == iota((GH, WIDE), 1) // DIM)
    mul_ref[...] = jnp.exp(dot(half8, by_head, TN, HIGHEST))

    r2_ref[...] = ones(iota((128, 512), 0) == iota((128, 512), 1) // GROUPS, BF16)
    r2t_ref[...] = ones(iota((512, 128), 1) == iota((512, 128), 0) // GROUPS, BF16)
    gmask_ref[...] = ones(iota((256, 512), 0) // DIM == iota((256, 512), 1) % GROUPS)
    low = iota((ROWS, ROWS), 0) // GROUPS >= iota((ROWS, ROWS), 1) // GROUPS
    low_ref[...] = ones(low)
    wmask_ref[...] = ones(low & (iota((ROWS, ROWS), 0) % GROUPS == iota((ROWS, ROWS), 1) % GROUPS))
    lane128 = iota((128, WIDE), 0)
    col128 = iota((128, WIDE), 1) // DIM
    eg = ones((lane128 // 64 == 0) & (lane128 % HEADS == col128), BF16)
    ex = ones((lane128 // 64 == 1) & (lane128 % HEADS == col128), BF16)
    mask4 = ones((iota((512, 128), 1) // HEADS) % GROUPS == iota((512, 128), 0) % GROUPS)
    rmask = ones(iota((512, 256), 0) % GROUPS == iota((512, 256), 1) // DIM)

    def pair_rows(i, k):
        return pl.ds(pl.multiple_of(i * 512 + k * 256, 256), 256)

    def pair_lanes(i):
        return pl.ds(pl.multiple_of(i * 128, 128), 128)

    def scale_pair(i, _):
        spread = dot(r2t_ref[...], st_ref[pair_lanes(i), :]) * mask4
        spread = spread.astype(BF16)
        b_pair, c_pair = bt_ref[:, pair_lanes(i)], ct_ref[:, pair_lanes(i)]
        bzt = (dot(b_pair, r2_ref[...]) * gmask_ref[...]).astype(BF16)
        czt = (dot(c_pair, r2_ref[...]) * gmask_ref[...]).astype(BF16)
        bz_ref[pl.ds(pl.multiple_of(i * 512, 512), 512), :] = (dot(r2t_ref[...], b_pair, NT) * rmask).astype(BF16)
        cz_ref[pl.ds(pl.multiple_of(i * 512, 512), 512), :] = (dot(r2t_ref[...], c_pair, NT) * rmask).astype(BF16)
        for k in range(2):
            part = spread[256 * k : 256 * k + 256]
            rows = pair_rows(i, k)
            tokens = pl.ds(i * 128 + k * 64, 64)
            scale = dot(part, ex)
            sx_ref[rows, :] = scale
            xt = (x_ref[tokens].reshape(ROWS, WIDE).astype(F32) * scale).astype(BF16)
            xt_ref[rows, :] = xt
            gt = (g_ref[tokens].reshape(ROWS, WIDE).astype(F32) * dot(part, eg)).astype(BF16)
            gt_ref[rows, :] = gt
            bz_k, cz_k = bzt[:, 256 * k : 256 * k + 256], czt[:, 256 * k : 256 * k + 256]
            bzt_ref[i * 2 + k] = bz_k
            czt_ref[i * 2 + k] = cz_k
            e_ref[i * 2 + k] = dot(bz_k, xt)
            f_ref[i * 2 + k] = dot(cz_k, gt)
        return 0

    lax.fori_loop(0, PAIRS, scale_pair, 0)

    def advance(state_ref, add_ref, c, low_out):
        for g in range(GROUPS):
            rows = slice(DIM * g, DIM * g + DIM)
            factor = mul_ref[pl.ds(c * GROUPS + g, 1), :]
            scaled = factor * state_ref[rows, :]
            if low_out is not None:
                low_out[c, rows, :] = scaled.astype(BF16)
            state_ref[rows, :] = factor * (scaled + add_ref[c, rows, :])

    def scan_chunks(s_low, g_low):
        def lap(c, _):
            advance(s_ref, e_ref, c, s_low)
            advance(g2_ref, f_ref, CHUNKS - 1 - c, g_low)
            return 0

        lax.fori_loop(0, CHUNKS, lap, 0)

    s_ref[...] = jnp.zeros_like(s_ref)
    g2_ref[...] = jnp.zeros_like(g2_ref)
    scan_chunks(None, None)
    for t in range(TILES):
        rows, lanes = slice(16 * (t // 4), 16 * (t // 4) + 16), slice(128 * (t % 4), 128 * (t % 4) + 128)
        snd1_ref[t // m, t % m, 0] = s_ref[rows, lanes].astype(BF16)
        snd1_ref[t // m, t % m, 1] = g2_ref[rows, lanes].astype(BF16)
    rcv1_ref[me] = snd1_ref[me]
    copy1 = functools.partial(to_peer, lambda peer: snd1_ref.at[peer], rcv1_ref, ss1, rs1)
    each_peer(lambda i: copy1(i).start())

    es_row = iota((WIDE, 128), 0) // DIM
    es_lane = iota((WIDE, 128), 1)

    def fold(kind):
        return ones((es_lane // GH == kind) & (es_lane % HEADS == es_row), BF16)

    def gather_rows(d, k):
        r = ones(iota((CHUNK, ROWS), 0) == iota((CHUNK, ROWS), 1) // GROUPS)
        return dot(r, d * mask4[:ROWS], precision=HIGHEST)

    def exact_fold(value, kind):
        hi = value.astype(BF16)
        lo = (value - hi.astype(F32)).astype(BF16)
        return dot(hi, fold(kind)) + dot(lo, fold(kind))

    def local_pair(i, _):
        gbs, gcs = [], []
        for k in range(2):
            c = i * 2 + k
            rows = pair_rows(i, k)
            xt, gt = xt_ref[rows, :], gt_ref[rows, :]
            bzt, czt = bzt_ref[c], czt_ref[c]
            mix = (dot(cz_ref[rows, :], bzt) * low_ref[...]).astype(BF16)
            mix_t = (dot(bz_ref[rows, :], czt) * low_ref[...].T).astype(BF16)
            y = dot(mix, xt)
            z = dot(mix_t, gt)
            z_ref[rows, :] = z
            d = exact_fold(gt.astype(F32) * y, 0) + exact_fold(xt.astype(F32) * z, 1)
            q_ref[pl.ds(i * 128 + k * 64, 64), :] = gather_rows(d, k)
            w = jnp.where(wmask_ref[...] > 0.5, dot(gt, xt, NT), 0.0).astype(BF16)
            gbs.append(dot(czt, w).astype(BF16))
            gcs.append(dot(bzt, w, NT).astype(BF16))
        gbacc_ref[:, pair_lanes(i)] = dot(jnp.concatenate(gbs, axis=1), r2t_ref[...])
        gcacc_ref[:, pair_lanes(i)] = dot(jnp.concatenate(gcs, axis=1), r2t_ref[...])
        return 0

    lax.fori_loop(0, PAIRS // 2, local_pair, 0)

    each_peer(lambda i: dec_copy(i).wait())
    each_peer(lambda i: copy1(i).wait())
    table = decall_ref[:, 0, :]
    for t in range(m):
        tile = me * m + t
        head = (tile // 16) * HEADS + (tile % 4) * 2 + sq1 // DIM
        decx_ref[t] = jnp.exp(dot(table, ones(sq0 == head), precision=HIGHEST))

    def lap(k, carry):
        back = n - 1 - k
        out = []
        for t in range(m):
            s, g = carry[2 * t], carry[2 * t + 1]
            snd2_ref[k, t, 0] = s.astype(BF16)
            snd2_ref[back, t, 1] = g.astype(BF16)
            s = decx_ref[t, pl.ds(k, 1), :] * s + rcv1_ref[k, t, 0].astype(F32)
            g = decx_ref[t, pl.ds(back, 1), :] * g + rcv1_ref[back, t, 1].astype(F32)
            out += [s, g]
        return tuple(out)

    lax.fori_loop(0, n, lap, tuple(jnp.zeros((16, 128), F32) for _ in range(2 * m)))
    rcv2_ref[me] = snd2_ref[me]
    copy2 = functools.partial(to_peer, lambda peer: snd2_ref.at[peer], rcv2_ref, ss2, rs2)
    each_peer(lambda i: copy2(i).start())

    lax.fori_loop(PAIRS // 2, PAIRS, local_pair, 0)

    each_peer(lambda i: copy2(i).wait())
    for t in range(TILES):
        rows, lanes = slice(16 * (t // 4), 16 * (t // 4) + 16), slice(128 * (t % 4), 128 * (t % 4) + 128)
        s_ref[rows, lanes] = rcv2_ref[t // m, t % m, 0].astype(F32)
        g2_ref[rows, lanes] = rcv2_ref[t // m, t % m, 1].astype(F32)
    scan_chunks(sp_ref, gp_ref)

    def cross_pair(i, _):
        gbs, gcs = [], []
        for k in range(2):
            c = i * 2 + k
            rows = pair_rows(i, k)
            tokens = pl.ds(i * 128 + k * 64, 64)
            xt, gt = xt_ref[rows, :], gt_ref[rows, :]
            sp, gp = sp_ref[c], gp_ref[c]
            through = sp.astype(F32) * gp.astype(F32)
            for g in range(GROUPS):
                part = jnp.sum(through[DIM * g : DIM * g + DIM], axis=0, keepdims=True)
                th_ref[pl.ds(c * GROUPS + g, 1), :] = part
            out = dot(cz_ref[rows, :], sp)
            back = dot(bz_ref[rows, :], gp)
            d = dot((gt.astype(F32) * out).astype(BF16), fold(0)) + dot((xt.astype(F32) * back).astype(BF16), fold(2))
            q_ref[tokens, :] = q_ref[tokens, :] + gather_rows(d, k)
            gin = (sx_ref[rows, :] * (z_ref[rows, :] + back)).astype(BF16)
            gin_ref[tokens] = gin.reshape(CHUNK, GROUPS, WIDE)
            gbs.append((dot(gp, xt, NT) * gmask_ref[:, :256]).astype(BF16))
            gcs.append((dot(sp, gt, NT) * gmask_ref[:, :256]).astype(BF16))
        gbacc_ref[:, pair_lanes(i)] = gbacc_ref[:, pair_lanes(i)] + dot(jnp.concatenate(gbs, axis=1), r2t_ref[...])
        gcacc_ref[:, pair_lanes(i)] = gcacc_ref[:, pair_lanes(i)] + dot(jnp.concatenate(gcs, axis=1), r2t_ref[...])
        return 0

    lax.fori_loop(0, PAIRS, cross_pair, 0)

    theirs = pl.ds(pl.multiple_of(other * 128, 128), 128)
    mine = pl.ds(pl.multiple_of(core * 128, 128), 128)
    tsnd_ref[0] = gbacc_ref[theirs, :].astype(BF16)
    tsnd_ref[1] = gcacc_ref[theirs, :].astype(BF16)
    swap = pltpu.make_async_remote_copy(
        src_ref=tsnd_ref, dst_ref=trcv_ref, send_sem=st4, recv_sem=rt4, device_id=(me, other), device_id_type=MESH
    )
    swap.start()

    qt = jnp.concatenate([q_ref[128 * j : 128 * j + 128, :].T for j in range(TOK // 128)], axis=1)
    inner, local, outer = qt[0:GH], qt[GH : 2 * GH], qt[2 * GH : 3 * GH]
    th = dot(th_ref[...], ones(iota((WIDE, GH), 0) // DIM == iota((WIDE, GH), 1) % HEADS), precision=HIGHEST)
    th = jnp.where(iota((32, GH), 0) % GROUPS == iota((32, GH), 1) // HEADS, th, 0.0)
    spread_th = ones(iota((32, TOK), 0) // GROUPS == iota((32, TOK), 1) // CHUNK)
    suffix = ones(same & (sq0 >= sq1))
    before = ones(same & (sq0 < sq1))
    log_grad = (
        along_tokens(inner - local, suffix) + along_tokens(outer, before) + dot(th, spread_th, TN, HIGHEST)
    )
    sig = 1.0 / (1.0 + jnp.exp(-u))
    graw = ((local + outer) / step - rates * log_grad) * sig
    graw_ref[...] = graw
    alog_col = jnp.sum(log_grad * ld, axis=1, keepdims=True)
    bias_col = jnp.sum(graw, axis=1, keepdims=True)
    pick = iota((GH, 128), 0) == iota((GH, 128), 1)
    alog_row = jnp.sum(jnp.where(pick, alog_col, 0.0), axis=0, keepdims=True)
    bias_row = jnp.sum(jnp.where(pick, bias_col, 0.0), axis=0, keepdims=True)
    tail_ref[...] = jnp.where(iota((8, 128), 0) < 4, alog_row, bias_row)
    tailall_ref[me] = tail_ref[...]
    tail_copy = functools.partial(to_peer, lambda peer: tail_ref, tailall_ref, ss3, rs3)
    each_peer(lambda i: tail_copy(i).start())

    swap.wait()
    gb_ref[...] = (gbacc_ref[mine, :] + trcv_ref[0].astype(F32)).astype(BF16)
    gc_ref[...] = (gcacc_ref[mine, :] + trcv_ref[1].astype(F32)).astype(BF16)

    each_peer(lambda i: tail_copy(i).wait())
    sums = jnp.sum(tailall_ref[...], axis=0)
    sums = jnp.where(iota((8, 128), 1) // HEADS == iota((8, 128), 0) % GROUPS, sums, 0.0)
    ends = dot(sums, ones(iota((128, HEADS), 0) % HEADS == iota((128, HEADS), 1)), precision=HIGHEST)
    galog_ref[...] = ends[0:4]
    gbias_ref[...] = ends[4:8]


def scratch(n):
    m = TILES // n
    dma = pltpu.SemaphoreType.DMA
    vm = pltpu.VMEM
    return [
        vm((TOK, 128), BF16), vm((2048, WIDE), F32), vm((2048, WIDE), BF16), vm((2048, WIDE), BF16),
        vm((CHUNKS, 256, 256), BF16), vm((CHUNKS, 256, 256), BF16), vm((2048, 256), BF16), vm((2048, 256), BF16),
        vm((CHUNKS, 256, WIDE), F32), vm((CHUNKS, 256, WIDE), F32), vm((32, WIDE), F32),
        vm((256, WIDE), F32), vm((256, WIDE), F32), vm((CHUNKS, 256, WIDE), BF16), vm((CHUNKS, 256, WIDE), BF16),
        vm((2048, WIDE), F32), vm((TOK, 128), F32), vm((256, TOK), F32), vm((256, TOK), F32), vm((32, WIDE), F32),
        vm((128, 512), BF16), vm((512, 128), BF16), vm((256, 512), F32), vm((ROWS, ROWS), F32), vm((ROWS, ROWS), F32),
        vm((8, 128), F32), vm((n, 8, 128), F32), vm((m, n, 128), F32),
        vm((n, m, 2, 16, 128), BF16), vm((n, m, 2, 16, 128), BF16), vm((n, m, 2, 16, 128), BF16), vm((n, m, 2, 16, 128), BF16),
        vm((2, 128, TOK), BF16), vm((2, 128, TOK), BF16), vm((8, 128), F32), vm((n, 8, 128), F32),
        dma((n,)), dma((n,)), dma((n,)), dma((n,)), dma((n,)), dma((n,)), dma((n,)), dma((n,)), dma, dma,
    ]


def solution(mesh):
    n = mesh.shape["ctx"]

    def body(inputs, grad_out, dt_raw, dt_bias, a_log, b_proj, c_proj):
        bt = jnp.transpose(b_proj, (1, 2, 0)).reshape(GROUPS * DIM, TOK)
        ct = jnp.transpose(c_proj, (1, 2, 0)).reshape(GROUPS * DIM, TOK)
        vmem = pl.BlockSpec(memory_space=pltpu.VMEM)
        gin, graw, galog, gbias, gb, gc = pl.pallas_call(
            functools.partial(kernel, n),
            out_shape=[
                jax.ShapeDtypeStruct((TOK, GROUPS, WIDE), BF16),
                jax.ShapeDtypeStruct((GH, TOK), F32),
                jax.ShapeDtypeStruct((GROUPS, HEADS), F32),
                jax.ShapeDtypeStruct((GROUPS, HEADS), F32),
                jax.ShapeDtypeStruct((128, TOK), BF16),
                jax.ShapeDtypeStruct((128, TOK), BF16),
            ],
            in_specs=[vmem] * 7,
            out_specs=[vmem] * 6,
            scratch_shapes=scratch(n),
            compiler_params=pltpu.CompilerParams(
                collective_id=0, has_side_effects=True, vmem_limit_bytes=58 * 2**20
            ),
        )(inputs, grad_out, dt_raw.reshape(GH, TOK), dt_bias, a_log, bt, ct)
        graw = graw.reshape(GROUPS, HEADS, TOK)
        gb = jnp.transpose(gb.reshape(2, DIM, TOK), (2, 0, 1))
        gc = jnp.transpose(gc.reshape(2, DIM, TOK), (2, 0, 1))
        return gin, graw, galog, gbias, gb, gc

    in_specs = (
        P("ctx", None, "tp"),
        P("ctx", None, "tp"),
        P(None, "tp", "ctx"),
        P(None, "tp"),
        P(None, "tp"),
        P("ctx", None, None),
        P("ctx", None, None),
    )
    out_specs = (
        P("ctx", None, "tp"),
        P(None, "tp", "ctx"),
        P(None, "tp"),
        P(None, "tp"),
        P("ctx", "tp", None),
        P("ctx", "tp", None),
    )
    return jax.shard_map(body, mesh=mesh, in_specs=in_specs, out_specs=out_specs, check_vma=False)
```

```python
import functools

import jax
import jax.numpy as jnp
from jax import lax
from jax.experimental import pallas as pl
from jax.experimental.pallas import tpu as pltpu
from jax.sharding import PartitionSpec as P

HIGHEST = lax.Precision.HIGHEST
F32 = jnp.float32
BF16 = jnp.bfloat16
MESH = pl.DeviceIdType.MESH

TOK = 512
GROUPS = 4
HEADS = 8
DIM = 64
CHUNK = 64
CHUNKS = TOK // CHUNK
PAIRS = CHUNKS // 2
ROWS = CHUNK * GROUPS
WIDE = HEADS * DIM
GH = GROUPS * HEADS
TILES = 64


def iota(shape, axis):
    return lax.broadcasted_iota(jnp.int32, shape, axis)


def over(value, size):
    return lax.shift_right_logical(value, size.bit_length() - 1)


def within(value, size):
    return value & (size - 1)


def ones(condition, kind=F32):
    return jnp.where(condition, 1.0, 0.0).astype(kind)


def dot(a, b, contract=((1,), (0,)), precision=None):
    return lax.dot_general(a, b, (contract, ((), ())), preferred_element_type=F32, precision=precision)


NT = ((1,), (1,))
TN = ((0,), (0,))


def kernel(
    n, x_hbm, g_hbm, dt_ref, bias_ref, alog_ref, bt_ref, ct_ref,
    gin_hbm, graw_ref, galog_ref, gbias_ref, gb_ref, gc_ref,
    x_ref, g_ref, gin_ref, st_ref, spread_ref, sx_ref, xt_ref, gt_ref, bzt_ref, czt_ref, bz_ref, cz_ref,
    e_ref, f_ref, mul_ref, s_ref, g2_ref, sp_ref, gp_ref, z_ref, lg_ref, al_ref, gbacc_ref, gcacc_ref, th_ref,
    step_ref, ld_ref, r2_ref, r2t_ref, low_ref, lowt_ref, wmask_ref,
    decsrc_ref, decall_ref, decx_ref, esnd_ref, ercv_ref, fsnd_ref, frcv_ref, ssnd_ref, srcv_ref, gsnd_ref, grcv_ref,
    tsnd_ref, trcv_ref, tail_ref, tailall_ref,
    ss0, rs0, sse, rse, ssf, rsf, sss, rss, ssg, rsg, ss3, rs3, st4, rt4, ld4, out4,
):
    m = TILES // n
    me = lax.axis_index("ctx")
    core = lax.axis_index("tp")
    other = 1 - core

    barrier = pltpu.get_barrier_semaphore()

    def greet(i, _):
        pl.semaphore_signal(barrier, inc=1, device_id=(lax.rem(me + i, n), core), device_id_type=MESH)
        return 0

    load_x = pltpu.make_async_copy(x_hbm, x_ref, ld4.at[0])
    load_g = pltpu.make_async_copy(g_hbm, g_ref, ld4.at[1])
    load_x.start()
    load_g.start()
    lax.fori_loop(1, n, greet, 0)
    pl.semaphore_signal(barrier, inc=1, device_id=(me, other), device_id_type=MESH)

    def to_peer(src, dst, ssem, rsem, i):
        peer = lax.rem(me + i, n)
        return pltpu.make_async_remote_copy(
            src_ref=src(peer), dst_ref=dst.at[me], send_sem=ssem, recv_sem=rsem,
            device_id=(peer, core), device_id_type=MESH,
        )

    def settle(dst, ssem, rsem):
        every = dst.at[pl.ds(0, n - 1)]
        pltpu.make_async_remote_copy(
            src_ref=every, dst_ref=every, send_sem=ssem, recv_sem=rsem,
            device_id=(me, other), device_id_type=MESH,
        ).wait()

    def each_peer(action):
        def lap(i, _):
            action(i)
            return 0

        lax.fori_loop(1, n, lap, 0)

    diag = iota((HEADS, HEADS), 0) == iota((HEADS, HEADS), 1)

    def column(ref):
        return jnp.concatenate(
            [jnp.sum(jnp.where(diag, ref[g : g + 1, :], 0.0), axis=1, keepdims=True) for g in range(GROUPS)], axis=0
        )

    rates = jnp.exp(column(alog_ref))
    u = dt_ref[...] + column(bias_ref)
    step = jnp.maximum(u, 0.0) + jnp.log1p(jnp.exp(-jnp.abs(u)))
    ld = -step * rates
    step_ref[...] = step
    ld_ref[...] = ld
    sq0, sq1 = iota((128, 128), 0), iota((128, 128), 1)
    same = over(sq0, CHUNK) == over(sq1, CHUNK)
    tri = ones(same & (sq0 <= sq1))
    block = ones(same)

    def along_tokens(value, table):
        return jnp.concatenate(
            [dot(value[:, 128 * j : 128 * j + 128], table, precision=HIGHEST) for j in range(TOK // 128)], axis=1
        )

    cum = along_tokens(ld, tri)
    half = along_tokens(ld, block) * 0.5
    sg = jnp.exp(cum - half)
    sx = step * jnp.exp(half - cum)
    sg_hi = sg.astype(BF16).astype(F32)
    sx_hi = sx.astype(BF16).astype(F32)
    stack = jnp.concatenate([sg_hi, sg - sg_hi, sx_hi, sx - sx_hi], axis=0)
    for j in range(TOK // 128):
        st_ref[128 * j : 128 * j + 128, :] = stack[:, 128 * j : 128 * j + 128].T.astype(BF16)

    total = jnp.sum(ld, axis=1, keepdims=True)
    row = jnp.sum(jnp.where(iota((GH, 128), 0) == iota((GH, 128), 1), total, 0.0), axis=0, keepdims=True)
    decsrc_ref[...] = row
    decall_ref[me] = decsrc_ref[...]

    first = ones(iota((TOK, CHUNKS * GROUPS), 0) == over(iota((TOK, CHUNKS * GROUPS), 1), GROUPS) * CHUNK)
    half8 = dot(half, first, precision=HIGHEST)
    half8 = jnp.where(over(iota((GH, 32), 0), HEADS) == within(iota((GH, 32), 1), GROUPS), half8, 0.0)
    by_head = ones(within(iota((GH, WIDE), 0), HEADS) == over(iota((GH, WIDE), 1), DIM))
    mul_ref[...] = jnp.exp(dot(half8, by_head, TN, HIGHEST))

    r2_ref[...] = ones(iota((128, 512), 0) == over(iota((128, 512), 1), GROUPS), BF16)
    r2t_ref[...] = ones(iota((512, 128), 1) == over(iota((512, 128), 0), GROUPS), BF16)
    gmask = ones(over(iota((256, 256), 0), DIM) == within(iota((256, 256), 1), GROUPS))
    lane128 = iota((128, WIDE), 0)
    col128 = over(iota((128, WIDE), 1), DIM)
    eg = ones((over(lane128, 64) == 0) & (within(lane128, HEADS) == col128), BF16)
    ex = ones((over(lane128, 64) == 1) & (within(lane128, HEADS) == col128), BF16)
    mask4 = ones(within(over(iota((ROWS, 128), 1), HEADS), GROUPS) == within(iota((ROWS, 128), 0), GROUPS))

    def pair_rows(i, k):
        return pl.ds(pl.multiple_of(i * 512 + k * 256, 256), 256)

    def pair_lanes(i):
        return pl.ds(pl.multiple_of(i * 128, 128), 128)

    def tokens_of(i, k):
        return pl.ds(i * 128 + k * 64, 64)

    def advance(state_ref, add_ref, c, low_out):
        for g in range(GROUPS):
            rows = slice(DIM * g, DIM * g + DIM)
            factor = mul_ref[pl.ds(c * GROUPS + g, 1), :]
            scaled = factor * state_ref[rows, :]
            if low_out is not None:
                low_out[c, rows, :] = scaled.astype(BF16)
            state_ref[rows, :] = factor * (scaled + add_ref[c, rows, :])

    def to_slices(state_ref, out_ref):
        for t in range(TILES):
            rows, lanes = slice(16 * (t // 4), 16 * (t // 4) + 16), slice(128 * (t % 4), 128 * (t % 4) + 128)
            out_ref[t // m, t % m] = state_ref[rows, lanes].astype(BF16)

    def from_slices(in_ref, state_ref):
        for t in range(TILES):
            rows, lanes = slice(16 * (t // 4), 16 * (t // 4) + 16), slice(128 * (t % 4), 128 * (t % 4) + 128)
            state_ref[rows, lanes] = in_ref[t // m, t % m].astype(F32)

    s_ref[...] = jnp.zeros_like(s_ref)
    g2_ref[...] = jnp.zeros_like(g2_ref)
    load_x.wait()

    def x_pair(i, _):
        bzt = dot(bt_ref[:, pair_lanes(i)], r2_ref[...])
        for k in range(2):
            rows = pair_rows(i, k)
            c = i * 2 + k
            part = (dot(r2t_ref[256 * k : 256 * k + 256, :], st_ref[pair_lanes(i), :]) * mask4).astype(BF16)
            spread_ref[rows, :] = part
            scale = dot(part, ex)
            sx_ref[rows, :] = scale
            xt = (x_ref[tokens_of(i, k)].reshape(ROWS, WIDE).astype(F32) * scale).astype(BF16)
            xt_ref[rows, :] = xt
            bz_k = (bzt[:, 256 * k : 256 * k + 256] * gmask).astype(BF16)
            bzt_ref[c] = bz_k
            e_ref[c] = dot(bz_k, xt)
            advance(s_ref, e_ref, c, None)
        return 0

    lax.fori_loop(0, PAIRS, x_pair, 0)
    to_slices(s_ref, esnd_ref)
    ercv_ref[me] = esnd_ref[me]
    pl.semaphore_wait(barrier, n)
    dec_copy = functools.partial(to_peer, lambda peer: decsrc_ref, decall_ref, ss0, rs0)
    each_peer(lambda i: dec_copy(i).start())
    copy_e = functools.partial(to_peer, lambda peer: esnd_ref.at[peer], ercv_ref, sse, rse)
    each_peer(lambda i: copy_e(i).start())

    load_g.wait()

    def g_pair(lap, _):
        i = PAIRS - 1 - lap
        czt = dot(ct_ref[:, pair_lanes(i)], r2_ref[...])
        for k in (1, 0):
            rows = pair_rows(i, k)
            c = i * 2 + k
            gt = (g_ref[tokens_of(i, k)].reshape(ROWS, WIDE).astype(F32) * dot(spread_ref[rows, :], eg)).astype(BF16)
            gt_ref[rows, :] = gt
            cz_k = (czt[:, 256 * k : 256 * k + 256] * gmask).astype(BF16)
            czt_ref[c] = cz_k
            f_ref[c] = dot(cz_k, gt)
            advance(g2_ref, f_ref, c, None)
        return 0

    lax.fori_loop(0, PAIRS, g_pair, 0)
    to_slices(g2_ref, fsnd_ref)
    frcv_ref[me] = fsnd_ref[me]
    copy_f = functools.partial(to_peer, lambda peer: fsnd_ref.at[peer], frcv_ref, ssf, rsf)
    each_peer(lambda i: copy_f(i).start())

    low = over(iota((ROWS, ROWS), 0), GROUPS) >= over(iota((ROWS, ROWS), 1), GROUPS)
    low_ref[...] = ones(low)
    lowt_ref[...] = ones(over(iota((ROWS, ROWS), 0), GROUPS) <= over(iota((ROWS, ROWS), 1), GROUPS))
    wmask_ref[...] = ones(low & (within(iota((ROWS, ROWS), 0), GROUPS) == within(iota((ROWS, ROWS), 1), GROUPS)))
    rmask = ones(within(iota((ROWS, 256), 0), GROUPS) == over(iota((ROWS, 256), 1), DIM))
    es_row = over(iota((WIDE, 128), 0), DIM)
    es_lane = iota((WIDE, 128), 1)
    fold_in = ones((over(es_lane, GH) == 0) & (within(es_lane, HEADS) == es_row), BF16)
    fold_out = ones((over(es_lane, GH) == 1) & (within(es_lane, HEADS) == es_row), BF16) - fold_in
    tr, tu = over(iota((512, 128), 0), GROUPS), iota((512, 128), 1)
    suffix = ones((tr >= tu) & (over(tr, CHUNK) == over(tu, CHUNK)), BF16)
    before = ones((tr < tu) & (over(tr, CHUNK) == over(tu, CHUNK)), BF16)
    plain = r2t_ref[...]
    suffix_plain = jnp.concatenate([suffix, plain], axis=1)
    before_plain = jnp.concatenate([before, plain], axis=1)

    def split(value):
        hi = value.astype(BF16)
        return hi, (value - hi.astype(F32)).astype(BF16)

    def exact_fold(value, table):
        hi, lo = split(value)
        return dot(hi, table) + dot(lo, table)

    def local_pair(i, _):
        gbs, gcs, ds = [], [], []
        b_pair, c_pair = bt_ref[:, pair_lanes(i)], ct_ref[:, pair_lanes(i)]
        for k in range(2):
            c = i * 2 + k
            rows = pair_rows(i, k)
            spread_t = r2t_ref[256 * k : 256 * k + 256, :]
            bz = (dot(spread_t, b_pair, NT) * rmask).astype(BF16)
            cz = (dot(spread_t, c_pair, NT) * rmask).astype(BF16)
            bz_ref[rows, :] = bz
            cz_ref[rows, :] = cz
            xt, gt = xt_ref[rows, :], gt_ref[rows, :]
            bzt, czt = bzt_ref[c], czt_ref[c]
            mix = (dot(cz, bzt) * low_ref[...]).astype(BF16)
            mix_t = (dot(bz, czt) * lowt_ref[...]).astype(BF16)
            y = dot(mix, xt)
            z = dot(mix_t, gt)
            z_ref[rows, :] = z
            d = exact_fold(gt.astype(F32) * y, fold_in) + exact_fold(xt.astype(F32) * z, fold_out)
            ds.append(d * mask4)
            w = jnp.where(wmask_ref[...] > 0.5, dot(gt, xt, NT), 0.0).astype(BF16)
            gbs.append(dot(czt, w).astype(BF16))
            gcs.append(dot(bzt, w, NT).astype(BF16))
        hi, lo = split(jnp.concatenate(ds, axis=0))
        sums = dot(hi, suffix_plain, TN) + dot(lo, suffix_plain, TN)
        lg_ref[:, pair_lanes(i)] = sums[0:GH, 0:128]
        al_ref[:, pair_lanes(i)] = sums[GH : 2 * GH, 128:256]
        gbacc_ref[:, pair_lanes(i)] = dot(jnp.concatenate(gbs, axis=1), r2t_ref[...])
        gcacc_ref[:, pair_lanes(i)] = dot(jnp.concatenate(gcs, axis=1), r2t_ref[...])
        return 0

    lax.fori_loop(0, 1, local_pair, 0)

    settle(decall_ref, ss0, rs0)
    settle(ercv_ref, sse, rse)
    table = decall_ref[...].reshape(n, 128)
    for t in range(m):
        tile = me * m + t
        head = (tile // 16) * HEADS + (tile % 4) * 2 + over(sq1, DIM)
        decx_ref[t] = jnp.exp(dot(table, ones(sq0 == head), precision=HIGHEST))

    def scan_blocks(in_ref, out_ref, place):
        def lap(step, carry):
            k = place(step)
            out = []
            for t in range(m):
                out_ref[k, t] = carry[t].astype(BF16)
                out.append(decx_ref[t, pl.ds(k, 1), :] * carry[t] + in_ref[k, t].astype(F32))
            return tuple(out)

        lax.fori_loop(0, n, lap, tuple(jnp.zeros((16, 128), F32) for _ in range(m)))

    scan_blocks(ercv_ref, ssnd_ref, lambda k: k)
    srcv_ref[me] = ssnd_ref[me]
    copy_s = functools.partial(to_peer, lambda peer: ssnd_ref.at[peer], srcv_ref, sss, rss)
    each_peer(lambda i: copy_s(i).start())

    lax.fori_loop(1, 2, local_pair, 0)

    settle(frcv_ref, ssf, rsf)
    scan_blocks(frcv_ref, gsnd_ref, lambda k: n - 1 - k)
    grcv_ref[me] = gsnd_ref[me]
    copy_g = functools.partial(to_peer, lambda peer: gsnd_ref.at[peer], grcv_ref, ssg, rsg)
    each_peer(lambda i: copy_g(i).start())

    lax.fori_loop(2, PAIRS, local_pair, 0)

    settle(srcv_ref, sss, rss)
    from_slices(srcv_ref, s_ref)

    def s_pair(i, _):
        gcs, ds = [], []
        for k in range(2):
            c = i * 2 + k
            rows = pair_rows(i, k)
            advance(s_ref, e_ref, c, sp_ref)
            gt, sp = gt_ref[rows, :], sp_ref[c]
            out = dot(cz_ref[rows, :], sp)
            ds.append((dot((gt.astype(F32) * out).astype(BF16), fold_in) * mask4).astype(BF16))
            gcs.append((dot(sp, gt, NT) * gmask).astype(BF16))
        sums = dot(jnp.concatenate(ds, axis=0), suffix, TN)
        lg_ref[:, pair_lanes(i)] = lg_ref[:, pair_lanes(i)] + sums[0:GH]
        gcacc_ref[:, pair_lanes(i)] = gcacc_ref[:, pair_lanes(i)] + dot(jnp.concatenate(gcs, axis=1), r2t_ref[...])
        return 0

    lax.fori_loop(0, PAIRS, s_pair, 0)

    theirs = pl.ds(pl.multiple_of(other * 128, 128), 128)
    mine = pl.ds(pl.multiple_of(core * 128, 128), 128)

    def swap(j):
        return pltpu.make_async_remote_copy(
            src_ref=tsnd_ref.at[j], dst_ref=trcv_ref.at[j], send_sem=st4.at[j], recv_sem=rt4.at[j],
            device_id=(me, other), device_id_type=MESH,
        )

    tsnd_ref[1] = gcacc_ref[theirs, :].astype(BF16)
    swap(1).start()

    settle(grcv_ref, ssg, rsg)
    from_slices(grcv_ref, g2_ref)

    def gin_copy(i):
        part = pl.ds(i * 128, 128)
        return pltpu.make_async_copy(gin_ref.at[part], gin_hbm.at[part], out4.at[i])

    def g_cross(lap, _):
        i = PAIRS - 1 - lap
        ds = [None, None]
        for k in (1, 0):
            c = i * 2 + k
            rows = pair_rows(i, k)
            advance(g2_ref, f_ref, c, gp_ref)
            gp = gp_ref[c]
            through = sp_ref[c].astype(F32) * gp.astype(F32)
            for g in range(GROUPS):
                part = jnp.sum(through[DIM * g : DIM * g + DIM], axis=0, keepdims=True)
                th_ref[pl.ds(c * GROUPS + g, 1), :] = part
            back = dot(bz_ref[rows, :], gp)
            ds[k] = (dot((xt_ref[rows, :].astype(F32) * back).astype(BF16), fold_in) * mask4).astype(BF16)
            gin = (sx_ref[rows, :] * (z_ref[rows, :] + back)).astype(BF16)
            gin_ref[tokens_of(i, k)] = gin.reshape(CHUNK, GROUPS, WIDE)
        gin_copy(i).start()
        sums = dot(jnp.concatenate(ds, axis=0), before_plain, TN)
        lg_ref[:, pair_lanes(i)] = lg_ref[:, pair_lanes(i)] + sums[0:GH, 0:128]
        al_ref[:, pair_lanes(i)] = al_ref[:, pair_lanes(i)] + sums[0:GH, 128:256]
        return 0

    lax.fori_loop(0, PAIRS, g_cross, 0)

    th = dot(th_ref[...], ones(over(iota((WIDE, GH), 0), DIM) == within(iota((WIDE, GH), 1), HEADS)), precision=HIGHEST)
    th = jnp.where(within(iota((32, GH), 0), GROUPS) == over(iota((32, GH), 1), HEADS), th, 0.0)
    spread_th = ones(over(iota((32, TOK), 0), GROUPS) == over(iota((32, TOK), 1), CHUNK))
    log_grad = lg_ref[...] + dot(th, spread_th, TN, HIGHEST)
    late_rates = jnp.exp(column(alog_ref))
    late_u = dt_ref[...] + column(bias_ref)
    sig = 1.0 / (1.0 + jnp.exp(-late_u))
    graw = (al_ref[...] / step_ref[...] - late_rates * log_grad) * sig
    graw_ref[...] = graw
    alog_col = jnp.sum(log_grad * ld_ref[...], axis=1, keepdims=True)
    bias_col = jnp.sum(graw, axis=1, keepdims=True)
    pick = iota((GH, 128), 0) == iota((GH, 128), 1)
    alog_row = jnp.sum(jnp.where(pick, alog_col, 0.0), axis=0, keepdims=True)
    bias_row = jnp.sum(jnp.where(pick, bias_col, 0.0), axis=0, keepdims=True)
    tail_ref[...] = alog_row + pltpu.roll(bias_row, GH, 1)
    tailall_ref[me] = tail_ref[...]
    tail_copy = functools.partial(to_peer, lambda peer: tail_ref, tailall_ref, ss3, rs3)
    each_peer(lambda i: tail_copy(i).start())

    def b_pair(i, _):
        gbs = []
        for k in range(2):
            gbs.append((dot(gp_ref[i * 2 + k], xt_ref[pair_rows(i, k), :], NT) * gmask).astype(BF16))
        gbacc_ref[:, pair_lanes(i)] = gbacc_ref[:, pair_lanes(i)] + dot(jnp.concatenate(gbs, axis=1), r2t_ref[...])
        return 0

    lax.fori_loop(0, PAIRS, b_pair, 0)
    tsnd_ref[0] = gbacc_ref[theirs, :].astype(BF16)
    swap(0).start()
    swap(1).wait()
    gc_ref[...] = (gcacc_ref[mine, :] + trcv_ref[1].astype(F32)).astype(BF16)
    swap(0).wait()
    gb_ref[...] = (gbacc_ref[mine, :] + trcv_ref[0].astype(F32)).astype(BF16)
    for i in range(PAIRS):
        gin_copy(i).wait()

    settle(tailall_ref, ss3, rs3)
    sums = jnp.sum(tailall_ref[...].reshape(n, 128), axis=0, keepdims=True)
    sums = jnp.where(over(iota((8, 128), 1), HEADS) == iota((8, 128), 0), sums, 0.0)
    ends = dot(sums, ones(within(iota((128, HEADS), 0), HEADS) == iota((128, HEADS), 1)), precision=HIGHEST)
    galog_ref[...] = ends[0:4]
    gbias_ref[...] = ends[4:8]


def hand_over(*refs):
    big_in, big_out, held, ins, outs = refs[0], refs[6], refs[12], refs[13], refs[14]
    parts = [pl.ds(128 * i, 128) for i in range(PAIRS)]
    loads = [pltpu.make_async_copy(big_in.at[p], held.at[p], ins.at[i]) for i, p in enumerate(parts)]
    stores = [pltpu.make_async_copy(held.at[p], big_out.at[p], outs.at[i]) for i, p in enumerate(parts)]
    for load in loads:
        load.start()
    for j in range(1, 6):
        refs[6 + j][...] = refs[j][...]
    for load, store in zip(loads, stores):
        load.wait()
        store.start()
    for store in stores:
        store.wait()


def scratch(n):
    m = TILES // n
    dma = pltpu.SemaphoreType.DMA
    vm = pltpu.VMEM
    slices = (n, m, 16, 128)
    return [
        vm((TOK, GROUPS, WIDE), BF16), vm((TOK, GROUPS, WIDE), BF16), vm((TOK, GROUPS, WIDE), BF16),
        vm((TOK, 128), BF16), vm((2048, 128), BF16), vm((2048, WIDE), F32), vm((2048, WIDE), BF16), vm((2048, WIDE), BF16),
        vm((CHUNKS, 256, 256), BF16), vm((CHUNKS, 256, 256), BF16), vm((2048, 256), BF16), vm((2048, 256), BF16),
        vm((CHUNKS, 256, WIDE), F32), vm((CHUNKS, 256, WIDE), F32), vm((32, WIDE), F32),
        vm((256, WIDE), F32), vm((256, WIDE), F32), vm((CHUNKS, 256, WIDE), BF16), vm((CHUNKS, 256, WIDE), BF16),
        vm((2048, WIDE), F32), vm((GH, TOK), F32), vm((GH, TOK), F32), vm((256, TOK), F32), vm((256, TOK), F32),
        vm((32, WIDE), F32), vm((GH, TOK), F32), vm((GH, TOK), F32),
        vm((128, 512), BF16), vm((512, 128), BF16), vm((ROWS, ROWS), F32), vm((ROWS, ROWS), F32), vm((ROWS, ROWS), F32),
        vm((1, 128), F32), vm((n, 1, 128), F32), vm((m, n, 128), F32),
        vm(slices, BF16), vm(slices, BF16), vm(slices, BF16), vm(slices, BF16),
        vm(slices, BF16), vm(slices, BF16), vm(slices, BF16), vm(slices, BF16),
        vm((2, 128, TOK), BF16), vm((2, 128, TOK), BF16), vm((1, 128), F32), vm((n, 1, 128), F32),
        dma, dma, dma, dma, dma, dma, dma, dma, dma, dma, dma, dma, dma((2,)), dma((2,)), dma((2,)), dma((PAIRS,)),
    ]


def solution(mesh):
    n = mesh.shape["ctx"]

    def body(inputs, grad_out, dt_raw, dt_bias, a_log, b_proj, c_proj):
        bt = jnp.transpose(b_proj, (1, 2, 0)).reshape(GROUPS * DIM, TOK)
        ct = jnp.transpose(c_proj, (1, 2, 0)).reshape(GROUPS * DIM, TOK)
        vmem = pl.BlockSpec(memory_space=pltpu.VMEM)
        hbm = pl.BlockSpec(memory_space=pl.ANY)
        shapes = [
            jax.ShapeDtypeStruct((TOK, GROUPS, WIDE), BF16),
            jax.ShapeDtypeStruct((GH, TOK), F32),
            jax.ShapeDtypeStruct((GROUPS, HEADS), F32),
            jax.ShapeDtypeStruct((GROUPS, HEADS), F32),
            jax.ShapeDtypeStruct((128, TOK), BF16),
            jax.ShapeDtypeStruct((128, TOK), BF16),
        ]
        results = pl.pallas_call(
            functools.partial(kernel, n),
            out_shape=shapes,
            in_specs=[hbm] * 2 + [vmem] * 5,
            out_specs=[hbm] + [vmem] * 5,
            scratch_shapes=scratch(n),
            compiler_params=pltpu.CompilerParams(
                collective_id=0, has_side_effects=True, vmem_limit_bytes=58 * 2**20
            ),
        )(inputs, grad_out, dt_raw.reshape(GH, TOK), dt_bias, a_log, bt, ct)
        gin, graw, galog, gbias, gb, gc = pl.pallas_call(
            hand_over,
            out_shape=shapes,
            in_specs=[hbm] + [vmem] * 5,
            out_specs=[hbm] + [vmem] * 5,
            scratch_shapes=[
                pltpu.VMEM((TOK, GROUPS, WIDE), BF16), pltpu.SemaphoreType.DMA((PAIRS,)), pltpu.SemaphoreType.DMA((PAIRS,)),
            ],
            compiler_params=pltpu.CompilerParams(vmem_limit_bytes=58 * 2**20),
        )(*results)
        graw = graw.reshape(GROUPS, HEADS, TOK)
        gb = jnp.transpose(gb.reshape(2, DIM, TOK), (2, 0, 1))
        gc = jnp.transpose(gc.reshape(2, DIM, TOK), (2, 0, 1))
        return gin, graw, galog, gbias, gb, gc

    in_specs = (
        P("ctx", None, "tp"),
        P("ctx", None, "tp"),
        P(None, "tp", "ctx"),
        P(None, "tp"),
        P(None, "tp"),
        P("ctx", None, None),
        P("ctx", None, None),
    )
    out_specs = (
        P("ctx", None, "tp"),
        P(None, "tp", "ctx"),
        P(None, "tp"),
        P(None, "tp"),
        P("ctx", "tp", None),
        P("ctx", "tp", None),
    )
    return jax.shard_map(body, mesh=mesh, in_specs=in_specs, out_specs=out_specs, check_vma=False)
```

```python
import functools

import jax
import jax.numpy as jnp
from jax import lax
from jax.experimental import pallas as pl
from jax.experimental.pallas import tpu as pltpu
from jax.sharding import PartitionSpec as P

F32 = jnp.float32
BF16 = jnp.bfloat16
MESH = pl.DeviceIdType.MESH

TOK = 512
GROUPS = 4
HEADS = 8
DIM = 64
CHUNK = 64
CHUNKS = TOK // CHUNK
PAIRS = CHUNKS // 2
ROWS = CHUNK * GROUPS
WIDE = HEADS * DIM
GH = GROUPS * HEADS
TILES = 64


def iota(shape, axis):
    return lax.broadcasted_iota(jnp.int32, shape, axis)


def over(value, size):
    return lax.shift_right_logical(value, size.bit_length() - 1)


def within(value, size):
    return value & (size - 1)


def ones(condition, kind=F32):
    return jnp.where(condition, 1.0, 0.0).astype(kind)


def dot(a, b, contract=((1,), (0,))):
    return lax.dot_general(a, b, (contract, ((), ())), preferred_element_type=F32)


NT = ((1,), (1,))
TN = ((0,), (0,))


def thirds(value):
    high = value.astype(BF16).astype(F32)
    middle = (value - high).astype(BF16).astype(F32)
    return jnp.concatenate([high, middle, value - high - middle], axis=0).astype(BF16)


def add_thirds(value):
    rows = value.shape[0] // 3
    return value[:rows] + value[rows : 2 * rows] + value[2 * rows :]


def far_first(n):
    if n != 64:
        return range(1, n)
    steps = [(i // 16, i // 4 % 4, i % 4) for i in range(1, n)]
    return sorted(steps, key=lambda step: -sum(min(way, 4 - way) for way in step))


def kernel(
    n, x_hbm, g_hbm, dt_ref, bias_ref, alog_ref, bt_ref, ct_ref,
    gin_ref, graw_ref, galog_ref, gbias_ref, gb_ref, gc_ref,
    x_ref, g_ref, st_ref, spread_ref, sx_ref, xt_ref, gt_ref, bzt_ref, czt_ref, bz_ref, cz_ref,
    e_ref, f_ref, mul_ref, s_ref, g2_ref, sp_ref, gp_ref, z_ref, wb_ref, wc_ref, lg_ref, al_ref, gbacc_ref, gcacc_ref, th_ref,
    step_ref, ld_ref, r2_ref, r2t_ref, low_ref, lowt_ref, wmask_ref,
    decsrc_ref, decall_ref, decx_ref, esnd_ref, ercv_ref, fsnd_ref, frcv_ref, ssnd_ref, srcv_ref, gsnd_ref, grcv_ref,
    tsnd_ref, trcv_ref, tail_ref, tailall_ref,
    ss0, rs0, sse, rse, ssf, rsf, sss, rss, ssg, rsg, ss3, rs3, st4, rt4, ld4,
):
    m = TILES // n
    me = lax.axis_index("ctx")
    core = lax.axis_index("tp")
    other = 1 - core

    barrier = pltpu.get_barrier_semaphore()

    def greet(i, _):
        pl.semaphore_signal(barrier, inc=1, device_id=(lax.rem(me + i, n), core), device_id_type=MESH)
        return 0

    load_x = pltpu.make_async_copy(x_hbm, x_ref, ld4.at[0])
    load_g = pltpu.make_async_copy(g_hbm, g_ref, ld4.at[1])
    load_x.start()
    load_g.start()
    lax.fori_loop(1, n, greet, 0)
    pl.semaphore_signal(barrier, inc=1, device_id=(me, other), device_id_type=MESH)

    def to_peer(src, dst, ssem, rsem, peer):
        return pltpu.make_async_remote_copy(
            src_ref=src(peer), dst_ref=dst.at[me], send_sem=ssem, recv_sem=rsem,
            device_id=(peer, core), device_id_type=MESH,
        )

    def settle(dst, ssem, rsem):
        every = dst.at[pl.ds(0, n - 1)]
        pltpu.make_async_remote_copy(
            src_ref=every, dst_ref=every, send_sem=ssem, recv_sem=rsem,
            device_id=(me, other), device_id_type=MESH,
        ).wait()

    def each_peer(action):
        for offset in far_first(n):
            if n == 64:
                spots = [lax.rem(lax.div(me, size) + step, 4) * size for size, step in zip((16, 4, 1), offset)]
                action(spots[0] + spots[1] + spots[2])
            else:
                action(lax.rem(me + offset, n))

    diag = iota((HEADS, HEADS), 0) == iota((HEADS, HEADS), 1)

    def column(ref):
        return jnp.concatenate(
            [jnp.sum(jnp.where(diag, ref[g : g + 1, :], 0.0), axis=1, keepdims=True) for g in range(GROUPS)], axis=0
        )

    rates = jnp.exp(column(alog_ref))
    u = dt_ref[...] + column(bias_ref)
    step = jnp.maximum(u, 0.0) + jnp.log1p(jnp.exp(-jnp.abs(u)))
    ld = -step * rates
    step_ref[...] = step
    ld_ref[...] = ld
    sq0, sq1 = iota((128, 128), 0), iota((128, 128), 1)
    same = over(sq0, CHUNK) == over(sq1, CHUNK)
    within_chunk = jnp.concatenate([ones(same & (sq0 <= sq1), BF16), ones(same, BF16)], axis=1)
    four = jnp.concatenate([ld[:, 128 * j : 128 * j + 128] for j in range(TOK // 128)], axis=0)
    sums = add_thirds(dot(thirds(four), within_chunk))
    cum = jnp.concatenate([sums[GH * j : GH * j + GH, 0:128] for j in range(TOK // 128)], axis=1)
    half = jnp.concatenate([sums[GH * j : GH * j + GH, 128:256] for j in range(TOK // 128)], axis=1) * 0.5
    sg = jnp.exp(cum - half)
    sx = step * jnp.exp(half - cum)
    sg_hi = sg.astype(BF16).astype(F32)
    sx_hi = sx.astype(BF16).astype(F32)
    stack = jnp.concatenate([sg_hi, sg - sg_hi, sx_hi, sx - sx_hi], axis=0)
    for j in range(TOK // 128):
        st_ref[128 * j : 128 * j + 128, :] = stack[:, 128 * j : 128 * j + 128].T.astype(BF16)

    total = jnp.sum(ld, axis=1, keepdims=True)
    row = jnp.sum(jnp.where(iota((GH, 128), 0) == iota((GH, 128), 1), total, 0.0), axis=0, keepdims=True)
    decsrc_ref[...] = row
    decall_ref[me] = decsrc_ref[...]

    chunk_of = ones(over(iota((TOK, CHUNKS * GROUPS), 0), CHUNK) == over(iota((TOK, CHUNKS * GROUPS), 1), GROUPS), BF16)
    half8 = add_thirds(dot(thirds(ld), chunk_of)) * 0.5
    half8 = jnp.where(over(iota((GH, 32), 0), HEADS) == within(iota((GH, 32), 1), GROUPS), half8, 0.0)
    by_head = ones(within(iota((3 * GH, WIDE), 0), HEADS) == over(iota((3 * GH, WIDE), 1), DIM), BF16)
    mul_ref[...] = jnp.exp(dot(thirds(half8), by_head, TN))

    r2_ref[...] = ones(iota((128, 512), 0) == over(iota((128, 512), 1), GROUPS), BF16)
    r2t_ref[...] = ones(iota((512, 128), 1) == over(iota((512, 128), 0), GROUPS), BF16)
    gmask = ones(over(iota((256, 256), 0), DIM) == within(iota((256, 256), 1), GROUPS))
    lane128 = iota((128, WIDE), 0)
    col128 = over(iota((128, WIDE), 1), DIM)
    eg = ones((over(lane128, 64) == 0) & (within(lane128, HEADS) == col128), BF16)
    ex = ones((over(lane128, 64) == 1) & (within(lane128, HEADS) == col128), BF16)
    mask4 = ones(within(over(iota((ROWS, 128), 1), HEADS), GROUPS) == within(iota((ROWS, 128), 0), GROUPS))

    def pair_rows(i, k):
        return pl.ds(pl.multiple_of(i * 512 + k * 256, 256), 256)

    def pair_lanes(i):
        return pl.ds(pl.multiple_of(i * 128, 128), 128)

    def tokens_of(i, k):
        return pl.ds(i * 128 + k * 64, 64)

    def each_pair(step):
        for i in range(PAIRS):
            step(i, 0)

    def twice(step):
        def lap(j, _):
            step(2 * j, 0)
            step(2 * j + 1, 0)
            return 0

        lax.fori_loop(0, PAIRS // 2, lap, 0)

    def advance(state_ref, add_ref, c, low_out):
        for g in range(GROUPS):
            rows = slice(DIM * g, DIM * g + DIM)
            factor = mul_ref[pl.ds(c * GROUPS + g, 1), :]
            scaled = factor * state_ref[rows, :]
            if low_out is not None:
                low_out[c, rows, :] = scaled.astype(BF16)
            add = add_ref[c, rows, :] if low_out is not None else add_ref[rows]
            state_ref[rows, :] = factor * (scaled + add)

    def to_slices(state_ref, out_ref):
        for t in range(TILES):
            rows, lanes = slice(16 * (t // 4), 16 * (t // 4) + 16), slice(128 * (t % 4), 128 * (t % 4) + 128)
            out_ref[t // m, t % m] = state_ref[rows, lanes].astype(BF16)

    def from_slices(in_ref, state_ref):
        for t in range(TILES):
            rows, lanes = slice(16 * (t // 4), 16 * (t // 4) + 16), slice(128 * (t % 4), 128 * (t % 4) + 128)
            state_ref[rows, lanes] = in_ref[t // m, t % m].astype(F32)

    s_ref[...] = jnp.zeros_like(s_ref)
    g2_ref[...] = jnp.zeros_like(g2_ref)
    load_x.wait()

    def x_pair(i, _):
        bzt = dot(bt_ref[:, pair_lanes(i)], r2_ref[...])
        for k in range(2):
            rows = pair_rows(i, k)
            c = i * 2 + k
            part = (dot(r2t_ref[256 * k : 256 * k + 256, :], st_ref[pair_lanes(i), :]) * mask4).astype(BF16)
            spread_ref[rows, :] = part
            scale = dot(part, ex)
            sx_ref[rows, :] = scale
            xt = (x_ref[tokens_of(i, k)].reshape(ROWS, WIDE).astype(F32) * scale).astype(BF16)
            xt_ref[rows, :] = xt
            bz_k = (bzt[:, 256 * k : 256 * k + 256] * gmask).astype(BF16)
            bzt_ref[c] = bz_k
            e = dot(bz_k, xt)
            e_ref[c] = e
            advance(s_ref, e, c, None)
        return 0

    each_pair(x_pair)
    to_slices(s_ref, esnd_ref)
    ercv_ref[me] = esnd_ref[me]
    pl.semaphore_wait(barrier, n)
    dec_copy = functools.partial(to_peer, lambda peer: decsrc_ref, decall_ref, ss0, rs0)
    each_peer(lambda i: dec_copy(i).start())
    copy_e = functools.partial(to_peer, lambda peer: esnd_ref.at[peer], ercv_ref, sse, rse)
    each_peer(lambda i: copy_e(i).start())

    load_g.wait()

    def g_pair(lap, _):
        i = PAIRS - 1 - lap
        czt = dot(ct_ref[:, pair_lanes(i)], r2_ref[...])
        for k in (1, 0):
            rows = pair_rows(i, k)
            c = i * 2 + k
            gt = (g_ref[tokens_of(i, k)].reshape(ROWS, WIDE).astype(F32) * dot(spread_ref[rows, :], eg)).astype(BF16)
            gt_ref[rows, :] = gt
            cz_k = (czt[:, 256 * k : 256 * k + 256] * gmask).astype(BF16)
            czt_ref[c] = cz_k
            f = dot(cz_k, gt)
            f_ref[c] = f
            advance(g2_ref, f, c, None)
        return 0

    twice(g_pair)
    to_slices(g2_ref, fsnd_ref)
    frcv_ref[me] = fsnd_ref[me]
    copy_f = functools.partial(to_peer, lambda peer: fsnd_ref.at[peer], frcv_ref, ssf, rsf)
    each_peer(lambda i: copy_f(i).start())

    low = over(iota((ROWS, ROWS), 0), GROUPS) >= over(iota((ROWS, ROWS), 1), GROUPS)
    low_ref[...] = ones(low)
    lowt_ref[...] = ones(over(iota((ROWS, ROWS), 0), GROUPS) <= over(iota((ROWS, ROWS), 1), GROUPS))
    wmask_ref[...] = ones(low & (within(iota((ROWS, ROWS), 0), GROUPS) == within(iota((ROWS, ROWS), 1), GROUPS)))
    rmask = ones(within(iota((ROWS, 256), 0), GROUPS) == over(iota((ROWS, 256), 1), DIM))
    es_row = over(iota((WIDE, 128), 0), DIM)
    es_lane = iota((WIDE, 128), 1)
    fold_in = ones((over(es_lane, GH) == 0) & (within(es_lane, HEADS) == es_row), BF16)
    fold_out = ones((over(es_lane, GH) == 1) & (within(es_lane, HEADS) == es_row), BF16)
    tr, tu = over(iota((512, 128), 0), GROUPS), iota((512, 128), 1)
    suffix = ones((tr >= tu) & (over(tr, CHUNK) == over(tu, CHUNK)), BF16)
    before = ones((tr < tu) & (over(tr, CHUNK) == over(tu, CHUNK)), BF16)
    plain = r2t_ref[...]
    suffix_plain = jnp.concatenate([suffix, plain], axis=1)
    before_plain = jnp.concatenate([before, plain], axis=1)

    def split(value):
        hi = value.astype(BF16)
        return hi, (value - hi.astype(F32)).astype(BF16)

    def local_pair(i, _):
        ds = []
        b_pair, c_pair = bt_ref[:, pair_lanes(i)], ct_ref[:, pair_lanes(i)]
        for k in range(2):
            c = i * 2 + k
            rows = pair_rows(i, k)
            spread_t = r2t_ref[256 * k : 256 * k + 256, :]
            bz = (dot(spread_t, b_pair, NT) * rmask).astype(BF16)
            cz = (dot(spread_t, c_pair, NT) * rmask).astype(BF16)
            bz_ref[rows, :] = bz
            cz_ref[rows, :] = cz
            xt, gt = xt_ref[rows, :], gt_ref[rows, :]
            bzt, czt = bzt_ref[c], czt_ref[c]
            mix = (dot(cz, bzt) * low_ref[...]).astype(BF16)
            mix_t = (dot(bz, czt) * lowt_ref[...]).astype(BF16)
            y = dot(mix, xt)
            z = dot(mix_t, gt)
            z_ref[rows, :] = z
            given = xt.astype(F32) * z
            kept = gt.astype(F32) * y - given
            hi, lo = split(kept)
            ds.append((dot(hi, fold_in) + dot(lo, fold_in) + dot(given.astype(BF16), fold_out)) * mask4)
            w = jnp.where(wmask_ref[...] > 0.5, dot(gt, xt, NT), 0.0).astype(BF16)
            wb_ref[c] = dot(czt, w).astype(BF16)
            wc_ref[c] = dot(bzt, w, NT).astype(BF16)
        hi, lo = split(jnp.concatenate(ds, axis=0))
        sums = dot(hi, suffix_plain, TN) + dot(lo, suffix_plain, TN)
        lg_ref[:, pair_lanes(i)] = sums[0:GH, 0:128]
        al_ref[:, pair_lanes(i)] = sums[GH : 2 * GH, 128:256]
        return 0

    lax.fori_loop(0, 1, local_pair, 0)

    settle(decall_ref, ss0, rs0)
    settle(ercv_ref, sse, rse)
    table = thirds(decall_ref[...].reshape(n, 128))
    for t in range(m):
        tile = me * m + t
        head = (tile // 16) * HEADS + (tile % 4) * 2 + over(sq1, DIM)
        decx_ref[t] = jnp.exp(add_thirds(dot(table, ones(sq0 == head, BF16))))

    def scan_blocks(in_ref, out_ref, place):
        width = 8 if n % 8 == 0 else 1

        def lap(step, carry):
            for j in range(width):
                k = place(step * width + j)
                out = []
                for t in range(m):
                    out_ref[k, t] = carry[t].astype(BF16)
                    out.append(decx_ref[t, pl.ds(k, 1), :] * carry[t] + in_ref[k, t].astype(F32))
                carry = tuple(out)
            return carry

        lax.fori_loop(0, n // width, lap, tuple(jnp.zeros((16, 128), F32) for _ in range(m)))

    scan_blocks(ercv_ref, ssnd_ref, lambda k: k)
    srcv_ref[me] = ssnd_ref[me]
    copy_s = functools.partial(to_peer, lambda peer: ssnd_ref.at[peer], srcv_ref, sss, rss)
    each_peer(lambda i: copy_s(i).start())

    lax.fori_loop(1, 2, local_pair, 0)

    settle(frcv_ref, ssf, rsf)
    scan_blocks(frcv_ref, gsnd_ref, lambda k: n - 1 - k)
    grcv_ref[me] = gsnd_ref[me]
    copy_g = functools.partial(to_peer, lambda peer: gsnd_ref.at[peer], grcv_ref, ssg, rsg)
    each_peer(lambda i: copy_g(i).start())

    lax.fori_loop(2, PAIRS, local_pair, 0)

    settle(srcv_ref, sss, rss)
    from_slices(srcv_ref, s_ref)

    def s_pair(i, _):
        ds = []
        for k in range(2):
            c = i * 2 + k
            rows = pair_rows(i, k)
            advance(s_ref, e_ref, c, sp_ref)
            gt, sp = gt_ref[rows, :], sp_ref[c]
            out = dot(cz_ref[rows, :], sp)
            ds.append(dot((gt.astype(F32) * out).astype(BF16), fold_in) * mask4)
        hi, lo = split(jnp.concatenate(ds, axis=0))
        sums = dot(hi, suffix, TN) + dot(lo, suffix, TN)
        lg_ref[:, pair_lanes(i)] = lg_ref[:, pair_lanes(i)] + sums[0:GH]
        return 0

    each_pair(s_pair)

    theirs = pl.ds(pl.multiple_of(other * 128, 128), 128)
    mine = pl.ds(pl.multiple_of(core * 128, 128), 128)

    swap = pltpu.make_async_remote_copy(
        src_ref=tsnd_ref, dst_ref=trcv_ref, send_sem=st4, recv_sem=rt4, device_id=(me, other), device_id_type=MESH
    )

    settle(grcv_ref, ssg, rsg)
    from_slices(grcv_ref, g2_ref)

    def g_cross(lap, _):
        i = PAIRS - 1 - lap
        ds = [None, None]
        for k in (1, 0):
            c = i * 2 + k
            rows = pair_rows(i, k)
            advance(g2_ref, f_ref, c, gp_ref)
            gp = gp_ref[c]
            through = sp_ref[c].astype(F32) * gp.astype(F32)
            for g in range(GROUPS):
                part = jnp.sum(through[DIM * g : DIM * g + DIM], axis=0, keepdims=True)
                th_ref[pl.ds(c * GROUPS + g, 1), :] = part
            back = dot(bz_ref[rows, :], gp)
            ds[k] = dot((xt_ref[rows, :].astype(F32) * back).astype(BF16), fold_in) * mask4
            e_ref[c] = back
        hi, lo = split(jnp.concatenate(ds, axis=0))
        sums = dot(hi, before_plain, TN) + dot(lo, before_plain, TN)
        lg_ref[:, pair_lanes(i)] = lg_ref[:, pair_lanes(i)] + sums[0:GH, 0:128]
        al_ref[:, pair_lanes(i)] = al_ref[:, pair_lanes(i)] + sums[0:GH, 128:256]
        return 0

    each_pair(g_cross)

    by_channel = ones(over(iota((WIDE, GH), 0), DIM) == within(iota((WIDE, GH), 1), HEADS), BF16)
    th = add_thirds(dot(thirds(th_ref[...]), by_channel))
    th = jnp.where(within(iota((32, GH), 0), GROUPS) == over(iota((32, GH), 1), HEADS), th, 0.0)
    spread_th = ones(over(iota((96, TOK), 0) & 31, GROUPS) == over(iota((96, TOK), 1), CHUNK), BF16)
    log_grad = lg_ref[...] + dot(thirds(th), spread_th, TN)
    late_rates = jnp.exp(column(alog_ref))
    late_u = dt_ref[...] + column(bias_ref)
    sig = 1.0 / (1.0 + jnp.exp(-late_u))
    graw = (al_ref[...] / step_ref[...] - late_rates * log_grad) * sig
    graw_ref[...] = graw
    alog_col = jnp.sum(log_grad * ld_ref[...], axis=1, keepdims=True)
    bias_col = jnp.sum(graw, axis=1, keepdims=True)
    pick = iota((GH, 128), 0) == iota((GH, 128), 1)
    alog_row = jnp.sum(jnp.where(pick, alog_col, 0.0), axis=0, keepdims=True)
    bias_row = jnp.sum(jnp.where(pick, bias_col, 0.0), axis=0, keepdims=True)
    tail_ref[...] = alog_row + pltpu.roll(bias_row, GH, 1)
    tailall_ref[me] = tail_ref[...]
    tail_copy = functools.partial(to_peer, lambda peer: tail_ref, tailall_ref, ss3, rs3)
    each_peer(lambda i: tail_copy(i).start())

    def bc_pair(i, _):
        gbs, gcs = [], []
        for k in range(2):
            c = i * 2 + k
            rows = pair_rows(i, k)
            gbs.append((wb_ref[c].astype(F32) + dot(gp_ref[c], xt_ref[rows, :], NT) * gmask).astype(BF16))
            gcs.append((wc_ref[c].astype(F32) + dot(sp_ref[c], gt_ref[rows, :], NT) * gmask).astype(BF16))
        gbacc_ref[:, pair_lanes(i)] = dot(jnp.concatenate(gbs, axis=1), r2t_ref[...])
        gcacc_ref[:, pair_lanes(i)] = dot(jnp.concatenate(gcs, axis=1), r2t_ref[...])
        return 0

    twice(bc_pair)
    tsnd_ref[0] = gbacc_ref[theirs, :].astype(BF16)
    tsnd_ref[1] = gcacc_ref[theirs, :].astype(BF16)
    swap.start()

    def gin_pair(i, _):
        for k in range(2):
            rows = pair_rows(i, k)
            gin = (sx_ref[rows, :] * (z_ref[rows, :] + e_ref[i * 2 + k])).astype(BF16)
            gin_ref[tokens_of(i, k)] = gin.reshape(CHUNK, GROUPS, WIDE)
        return 0

    lax.fori_loop(0, PAIRS, gin_pair, 0)
    swap.wait()
    gb_ref[...] = (gbacc_ref[mine, :] + trcv_ref[0].astype(F32)).astype(BF16)
    gc_ref[...] = (gcacc_ref[mine, :] + trcv_ref[1].astype(F32)).astype(BF16)

    settle(tailall_ref, ss3, rs3)
    sums = jnp.sum(tailall_ref[...].reshape(n, 128), axis=0, keepdims=True)
    sums = jnp.where(over(iota((8, 128), 1), HEADS) == iota((8, 128), 0), sums, 0.0)
    ends = add_thirds(dot(thirds(sums), ones(within(iota((128, HEADS), 0), HEADS) == iota((128, HEADS), 1), BF16)))
    galog_ref[...] = ends[0:4]
    gbias_ref[...] = ends[4:8]


def hand_over(*refs):
    ins, outs, sems = refs[:6], refs[6:12], refs[12]
    copies = [pltpu.make_async_copy(a, b, sems.at[j]) for j, (a, b) in enumerate(zip(ins, outs))]
    for copy in copies:
        copy.start()
    for copy in copies:
        copy.wait()


def scratch(n):
    m = TILES // n
    dma = pltpu.SemaphoreType.DMA
    vm = pltpu.VMEM
    slices = (n, m, 16, 128)
    return [
        vm((TOK, GROUPS, WIDE), BF16), vm((TOK, GROUPS, WIDE), BF16),
        vm((TOK, 128), BF16), vm((2048, 128), BF16), vm((2048, WIDE), F32), vm((2048, WIDE), BF16), vm((2048, WIDE), BF16),
        vm((CHUNKS, 256, 256), BF16), vm((CHUNKS, 256, 256), BF16), vm((2048, 256), BF16), vm((2048, 256), BF16),
        vm((CHUNKS, 256, WIDE), F32), vm((CHUNKS, 256, WIDE), F32), vm((32, WIDE), F32),
        vm((256, WIDE), F32), vm((256, WIDE), F32), vm((CHUNKS, 256, WIDE), BF16), vm((CHUNKS, 256, WIDE), BF16),
        vm((2048, WIDE), F32), vm((CHUNKS, 256, 256), BF16), vm((CHUNKS, 256, 256), BF16),
        vm((GH, TOK), F32), vm((GH, TOK), F32), vm((256, TOK), F32), vm((256, TOK), F32),
        vm((32, WIDE), F32), vm((GH, TOK), F32), vm((GH, TOK), F32),
        vm((128, 512), BF16), vm((512, 128), BF16), vm((ROWS, ROWS), F32), vm((ROWS, ROWS), F32), vm((ROWS, ROWS), F32),
        vm((1, 128), F32), vm((n, 1, 128), F32), vm((m, n, 128), F32),
        vm(slices, BF16), vm(slices, BF16), vm(slices, BF16), vm(slices, BF16),
        vm(slices, BF16), vm(slices, BF16), vm(slices, BF16), vm(slices, BF16),
        vm((2, 128, TOK), BF16), vm((2, 128, TOK), BF16), vm((1, 128), F32), vm((n, 1, 128), F32),
        dma, dma, dma, dma, dma, dma, dma, dma, dma, dma, dma, dma, dma, dma, dma((2,)),
    ]


def solution(mesh):
    n = mesh.shape["ctx"]

    def body(inputs, grad_out, dt_raw, dt_bias, a_log, b_proj, c_proj):
        bt = jnp.transpose(b_proj, (1, 2, 0)).reshape(GROUPS * DIM, TOK)
        ct = jnp.transpose(c_proj, (1, 2, 0)).reshape(GROUPS * DIM, TOK)
        vmem = pl.BlockSpec(memory_space=pltpu.VMEM)
        hbm = pl.BlockSpec(memory_space=pl.ANY)
        shapes = [
            jax.ShapeDtypeStruct((TOK, GROUPS, WIDE), BF16),
            jax.ShapeDtypeStruct((GH, TOK), F32),
            jax.ShapeDtypeStruct((GROUPS, HEADS), F32),
            jax.ShapeDtypeStruct((GROUPS, HEADS), F32),
            jax.ShapeDtypeStruct((128, TOK), BF16),
            jax.ShapeDtypeStruct((128, TOK), BF16),
        ]
        results = pl.pallas_call(
            functools.partial(kernel, n),
            out_shape=[pltpu.VMEM(shape.shape, shape.dtype) for shape in shapes],
            in_specs=[hbm] * 2 + [vmem] * 5,
            out_specs=[vmem] * 6,
            scratch_shapes=scratch(n),
            compiler_params=pltpu.CompilerParams(
                collective_id=0, has_side_effects=True, vmem_limit_bytes=56 * 2**20
            ),
        )(inputs, grad_out, dt_raw.reshape(GH, TOK), dt_bias, a_log, bt, ct)
        gin, graw, galog, gbias, gb, gc = pl.pallas_call(
            hand_over,
            out_shape=shapes,
            in_specs=[vmem] * 6,
            out_specs=[hbm] * 6,
            scratch_shapes=[pltpu.SemaphoreType.DMA((6,))],
            compiler_params=pltpu.CompilerParams(vmem_limit_bytes=4 * 2**20),
        )(*results)
        graw = graw.reshape(GROUPS, HEADS, TOK)
        gb = jnp.transpose(gb.reshape(2, DIM, TOK), (2, 0, 1))
        gc = jnp.transpose(gc.reshape(2, DIM, TOK), (2, 0, 1))
        return gin, graw, galog, gbias, gb, gc

    in_specs = (
        P("ctx", None, "tp"),
        P("ctx", None, "tp"),
        P(None, "tp", "ctx"),
        P(None, "tp"),
        P(None, "tp"),
        P("ctx", None, None),
        P("ctx", None, None),
    )
    out_specs = (
        P("ctx", None, "tp"),
        P(None, "tp", "ctx"),
        P(None, "tp"),
        P(None, "tp"),
        P("ctx", "tp", None),
        P("ctx", "tp", None),
    )
    return jax.shard_map(body, mesh=mesh, in_specs=in_specs, out_specs=out_specs, check_vma=False)
```

```python
import functools

import jax
import jax.numpy as jnp
from jax import lax
from jax.experimental import pallas as pl
from jax.experimental.pallas import tpu as pltpu
from jax.sharding import PartitionSpec as P

F32 = jnp.float32
BF16 = jnp.bfloat16
MESH = pl.DeviceIdType.MESH

TOK = 512
GROUPS = 4
HEADS = 8
DIM = 64
CHUNK = 64
CHUNKS = TOK // CHUNK
PAIRS = CHUNKS // 2
ROWS = CHUNK * GROUPS
WIDE = HEADS * DIM
GH = GROUPS * HEADS
TILES = 64


def iota(shape, axis):
    return lax.broadcasted_iota(jnp.int32, shape, axis)


def over(value, size):
    return lax.shift_right_logical(value, size.bit_length() - 1)


def within(value, size):
    return value & (size - 1)


def ones(condition, kind=F32):
    return jnp.where(condition, 1.0, 0.0).astype(kind)


def dot(a, b, contract=((1,), (0,))):
    return lax.dot_general(a, b, (contract, ((), ())), preferred_element_type=F32)


NT = ((1,), (1,))
TN = ((0,), (0,))


def thirds(value):
    high = value.astype(BF16).astype(F32)
    middle = (value - high).astype(BF16).astype(F32)
    return jnp.concatenate([high, middle, value - high - middle], axis=0).astype(BF16)


def add_thirds(value):
    rows = value.shape[0] // 3
    return value[:rows] + value[rows : 2 * rows] + value[2 * rows :]


def far_first(n):
    if n != 64:
        return range(1, n)
    steps = [(i // 16, i // 4 % 4, i % 4) for i in range(1, n)]
    return sorted(steps, key=lambda step: -sum(min(way, 4 - way) for way in step))


def kernel(
    n, x_hbm, g_hbm, dt_hbm, bias_hbm, alog_hbm, bt_hbm, ct_hbm,
    gin_ref, graw_ref, galog_ref, gbias_ref, gb_ref, gc_ref,
    x_ref, g_ref, dt_ref, bias_ref, alog_ref, bt_ref, ct_ref, st_ref, spread_ref, sx_ref, xt_ref, gt_ref, bzt_ref, czt_ref, bz_ref, cz_ref,
    e_ref, f_ref, mul_ref, s_ref, g2_ref, sp_ref, gp_ref, z_ref, wb_ref, wc_ref, lg_ref, al_ref, gbacc_ref, gcacc_ref, th_ref,
    step_ref, ld_ref, r2_ref, r2t_ref, low_ref, lowt_ref, wmask_ref,
    decsrc_ref, decall_ref, decx_ref, esnd_ref, ercv_ref, fsnd_ref, frcv_ref, ssnd_ref, srcv_ref, gsnd_ref, grcv_ref,
    tsnd_ref, trcv_ref, tail_ref, tailall_ref,
    ss0, rs0, sse, rse, ssf, rsf, sss, rss, ssg, rsg, ss3, rs3, st4, rt4, ld4,
):
    m = TILES // n
    me = lax.axis_index("ctx")
    core = lax.axis_index("tp")
    other = 1 - core

    barrier = pltpu.get_barrier_semaphore()

    def greet(i, _):
        pl.semaphore_signal(barrier, inc=1, device_id=(lax.rem(me + i, n), core), device_id_type=MESH)
        return 0

    homes = (dt_hbm, dt_ref), (bias_hbm, bias_ref), (alog_hbm, alog_ref), (x_hbm, x_ref), (bt_hbm, bt_ref), (g_hbm, g_ref), (ct_hbm, ct_ref)
    loads = [pltpu.make_async_copy(a, b, ld4.at[j]) for j, (a, b) in enumerate(homes)]
    for load in loads:
        load.start()
    lax.fori_loop(1, n, greet, 0)
    pl.semaphore_signal(barrier, inc=1, device_id=(me, other), device_id_type=MESH)

    def to_peer(src, dst, ssem, rsem, peer):
        return pltpu.make_async_remote_copy(
            src_ref=src(peer), dst_ref=dst.at[me], send_sem=ssem, recv_sem=rsem,
            device_id=(peer, core), device_id_type=MESH,
        )

    def settle(dst, ssem, rsem):
        every = dst.at[pl.ds(0, n - 1)]
        pltpu.make_async_remote_copy(
            src_ref=every, dst_ref=every, send_sem=ssem, recv_sem=rsem,
            device_id=(me, other), device_id_type=MESH,
        ).wait()

    def each_peer(action):
        for offset in far_first(n):
            if n == 64:
                spots = [lax.rem(lax.div(me, size) + step, 4) * size for size, step in zip((16, 4, 1), offset)]
                action(spots[0] + spots[1] + spots[2])
            else:
                action(lax.rem(me + offset, n))

    diag = iota((HEADS, HEADS), 0) == iota((HEADS, HEADS), 1)

    def column(ref):
        return jnp.concatenate(
            [jnp.sum(jnp.where(diag, ref[g : g + 1, :], 0.0), axis=1, keepdims=True) for g in range(GROUPS)], axis=0
        )

    for load in loads[:3]:
        load.wait()
    rates = jnp.exp(column(alog_ref))
    u = dt_ref[...] + column(bias_ref)
    step = jnp.maximum(u, 0.0) + jnp.log1p(jnp.exp(-jnp.abs(u)))
    ld = -step * rates
    step_ref[...] = step
    ld_ref[...] = ld
    sq0, sq1 = iota((128, 128), 0), iota((128, 128), 1)
    same = over(sq0, CHUNK) == over(sq1, CHUNK)
    within_chunk = jnp.concatenate([ones(same & (sq0 <= sq1), BF16), ones(same, BF16)], axis=1)
    four = jnp.concatenate([ld[:, 128 * j : 128 * j + 128] for j in range(TOK // 128)], axis=0)
    sums = add_thirds(dot(thirds(four), within_chunk))
    cum = jnp.concatenate([sums[GH * j : GH * j + GH, 0:128] for j in range(TOK // 128)], axis=1)
    half = jnp.concatenate([sums[GH * j : GH * j + GH, 128:256] for j in range(TOK // 128)], axis=1) * 0.5
    sg = jnp.exp(cum - half)
    sx = step * jnp.exp(half - cum)
    sg_hi = sg.astype(BF16).astype(F32)
    sx_hi = sx.astype(BF16).astype(F32)
    stack = jnp.concatenate([sg_hi, sg - sg_hi, sx_hi, sx - sx_hi], axis=0)
    for j in range(TOK // 128):
        st_ref[128 * j : 128 * j + 128, :] = stack[:, 128 * j : 128 * j + 128].T.astype(BF16)

    total = jnp.sum(ld, axis=1, keepdims=True)
    row = jnp.sum(jnp.where(iota((GH, 128), 0) == iota((GH, 128), 1), total, 0.0), axis=0, keepdims=True)
    decsrc_ref[...] = row
    decall_ref[me] = decsrc_ref[...]

    chunk_of = ones(over(iota((TOK, CHUNKS * GROUPS), 0), CHUNK) == over(iota((TOK, CHUNKS * GROUPS), 1), GROUPS), BF16)
    half8 = add_thirds(dot(thirds(ld), chunk_of)) * 0.5
    half8 = jnp.where(over(iota((GH, 32), 0), HEADS) == within(iota((GH, 32), 1), GROUPS), half8, 0.0)
    by_head = ones(within(iota((3 * GH, WIDE), 0), HEADS) == over(iota((3 * GH, WIDE), 1), DIM), BF16)
    mul_ref[...] = jnp.exp(dot(thirds(half8), by_head, TN))

    r2_ref[...] = ones(iota((128, 512), 0) == over(iota((128, 512), 1), GROUPS), BF16)
    r2t_ref[...] = ones(iota((512, 128), 1) == over(iota((512, 128), 0), GROUPS), BF16)
    gmask = ones(over(iota((256, 256), 0), DIM) == within(iota((256, 256), 1), GROUPS))
    lane128 = iota((128, WIDE), 0)
    col128 = over(iota((128, WIDE), 1), DIM)
    eg = ones((over(lane128, 64) == 0) & (within(lane128, HEADS) == col128), BF16)
    ex = ones((over(lane128, 64) == 1) & (within(lane128, HEADS) == col128), BF16)
    mask4 = ones(within(over(iota((ROWS, 128), 1), HEADS), GROUPS) == within(iota((ROWS, 128), 0), GROUPS))

    def pair_rows(i, k):
        return pl.ds(pl.multiple_of(i * 512 + k * 256, 256), 256)

    def pair_lanes(i):
        return pl.ds(pl.multiple_of(i * 128, 128), 128)

    def tokens_of(i, k):
        return pl.ds(i * 128 + k * 64, 64)

    def each_pair(step):
        for i in range(PAIRS):
            step(i, 0)

    def twice(step):
        def lap(j, _):
            step(2 * j, 0)
            step(2 * j + 1, 0)
            return 0

        lax.fori_loop(0, PAIRS // 2, lap, 0)

    def advance(state_ref, add_ref, c, low_out):
        for g in range(GROUPS):
            rows = slice(DIM * g, DIM * g + DIM)
            factor = mul_ref[pl.ds(c * GROUPS + g, 1), :]
            scaled = factor * state_ref[rows, :]
            if low_out is not None:
                low_out[c, rows, :] = scaled.astype(BF16)
            add = add_ref[c, rows, :] if low_out is not None else add_ref[rows]
            state_ref[rows, :] = factor * (scaled + add)

    def to_slices(state_ref, out_ref):
        for t in range(TILES):
            rows, lanes = slice(16 * (t // 4), 16 * (t // 4) + 16), slice(128 * (t % 4), 128 * (t % 4) + 128)
            out_ref[t // m, t % m] = state_ref[rows, lanes].astype(BF16)

    def from_slices(in_ref, state_ref):
        for t in range(TILES):
            rows, lanes = slice(16 * (t // 4), 16 * (t // 4) + 16), slice(128 * (t % 4), 128 * (t % 4) + 128)
            state_ref[rows, lanes] = in_ref[t // m, t % m].astype(F32)

    s_ref[...] = jnp.zeros_like(s_ref)
    g2_ref[...] = jnp.zeros_like(g2_ref)
    loads[3].wait()
    loads[4].wait()

    def x_pair(i, _):
        bzt = dot(bt_ref[:, pair_lanes(i)], r2_ref[...])
        for k in range(2):
            rows = pair_rows(i, k)
            c = i * 2 + k
            part = (dot(r2t_ref[256 * k : 256 * k + 256, :], st_ref[pair_lanes(i), :]) * mask4).astype(BF16)
            spread_ref[rows, :] = part
            scale = dot(part, ex)
            sx_ref[rows, :] = scale
            xt = (x_ref[tokens_of(i, k)].reshape(ROWS, WIDE).astype(F32) * scale).astype(BF16)
            xt_ref[rows, :] = xt
            bz_k = (bzt[:, 256 * k : 256 * k + 256] * gmask).astype(BF16)
            bzt_ref[c] = bz_k
            e = dot(bz_k, xt)
            e_ref[c] = e
            advance(s_ref, e, c, None)
        return 0

    each_pair(x_pair)
    to_slices(s_ref, esnd_ref)
    ercv_ref[me] = esnd_ref[me]
    pl.semaphore_wait(barrier, n)
    dec_copy = functools.partial(to_peer, lambda peer: decsrc_ref, decall_ref, ss0, rs0)
    each_peer(lambda i: dec_copy(i).start())
    copy_e = functools.partial(to_peer, lambda peer: esnd_ref.at[peer], ercv_ref, sse, rse)
    each_peer(lambda i: copy_e(i).start())

    loads[5].wait()
    loads[6].wait()

    def g_pair(lap, _):
        i = PAIRS - 1 - lap
        czt = dot(ct_ref[:, pair_lanes(i)], r2_ref[...])
        for k in (1, 0):
            rows = pair_rows(i, k)
            c = i * 2 + k
            gt = (g_ref[tokens_of(i, k)].reshape(ROWS, WIDE).astype(F32) * dot(spread_ref[rows, :], eg)).astype(BF16)
            gt_ref[rows, :] = gt
            cz_k = (czt[:, 256 * k : 256 * k + 256] * gmask).astype(BF16)
            czt_ref[c] = cz_k
            f = dot(cz_k, gt)
            f_ref[c] = f
            advance(g2_ref, f, c, None)
        return 0

    each_pair(g_pair)
    to_slices(g2_ref, fsnd_ref)
    frcv_ref[me] = fsnd_ref[me]
    copy_f = functools.partial(to_peer, lambda peer: fsnd_ref.at[peer], frcv_ref, ssf, rsf)
    each_peer(lambda i: copy_f(i).start())

    low = over(iota((ROWS, ROWS), 0), GROUPS) >= over(iota((ROWS, ROWS), 1), GROUPS)
    low_ref[...] = ones(low)
    lowt_ref[...] = ones(over(iota((ROWS, ROWS), 0), GROUPS) <= over(iota((ROWS, ROWS), 1), GROUPS))
    wmask_ref[...] = ones(low & (within(iota((ROWS, ROWS), 0), GROUPS) == within(iota((ROWS, ROWS), 1), GROUPS)))
    rmask = ones(within(iota((ROWS, 256), 0), GROUPS) == over(iota((ROWS, 256), 1), DIM))
    es_row = over(iota((WIDE, 128), 0), DIM)
    es_lane = iota((WIDE, 128), 1)
    fold_in = ones((over(es_lane, GH) == 0) & (within(es_lane, HEADS) == es_row), BF16)
    fold_out = ones((over(es_lane, GH) == 1) & (within(es_lane, HEADS) == es_row), BF16)
    tr, tu = over(iota((512, 128), 0), GROUPS), iota((512, 128), 1)
    suffix = ones((tr >= tu) & (over(tr, CHUNK) == over(tu, CHUNK)), BF16)
    before = ones((tr < tu) & (over(tr, CHUNK) == over(tu, CHUNK)), BF16)
    plain = r2t_ref[...]
    suffix_plain = jnp.concatenate([suffix, plain], axis=1)
    before_plain = jnp.concatenate([before, plain], axis=1)

    def split(value):
        hi = value.astype(BF16)
        return hi, (value - hi.astype(F32)).astype(BF16)

    def local_pair(i, _):
        ds = []
        b_pair, c_pair = bt_ref[:, pair_lanes(i)], ct_ref[:, pair_lanes(i)]
        for k in range(2):
            c = i * 2 + k
            rows = pair_rows(i, k)
            spread_t = r2t_ref[256 * k : 256 * k + 256, :]
            bz = (dot(spread_t, b_pair, NT) * rmask).astype(BF16)
            cz = (dot(spread_t, c_pair, NT) * rmask).astype(BF16)
            bz_ref[rows, :] = bz
            cz_ref[rows, :] = cz
            xt, gt = xt_ref[rows, :], gt_ref[rows, :]
            bzt, czt = bzt_ref[c], czt_ref[c]
            mix = (dot(cz, bzt) * low_ref[...]).astype(BF16)
            mix_t = (dot(bz, czt) * lowt_ref[...]).astype(BF16)
            y = dot(mix, xt)
            z = dot(mix_t, gt)
            z_ref[rows, :] = z
            given = xt.astype(F32) * z
            kept = gt.astype(F32) * y - given
            hi, lo = split(kept)
            ds.append((dot(hi, fold_in) + dot(lo, fold_in) + dot(given.astype(BF16), fold_out)) * mask4)
            w = jnp.where(wmask_ref[...] > 0.5, dot(gt, xt, NT), 0.0).astype(BF16)
            wb_ref[c] = dot(czt, w).astype(BF16)
            wc_ref[c] = dot(bzt, w, NT).astype(BF16)
        hi, lo = split(jnp.concatenate(ds, axis=0))
        sums = dot(hi, suffix_plain, TN) + dot(lo, suffix_plain, TN)
        lg_ref[:, pair_lanes(i)] = sums[0:GH, 0:128]
        al_ref[:, pair_lanes(i)] = sums[GH : 2 * GH, 128:256]
        return 0

    lax.fori_loop(0, 1, local_pair, 0)

    settle(decall_ref, ss0, rs0)
    settle(ercv_ref, sse, rse)
    table = thirds(decall_ref[...].reshape(n, 128))
    for t in range(m):
        tile = me * m + t
        head = (tile // 16) * HEADS + (tile % 4) * 2 + over(sq1, DIM)
        decx_ref[t] = jnp.exp(add_thirds(dot(table, ones(sq0 == head, BF16))))

    def scan_blocks(in_ref, out_ref, place):
        width = 8 if n % 8 == 0 else 1

        def lap(step, carry):
            for j in range(width):
                k = place(step * width + j)
                out = []
                for t in range(m):
                    out_ref[k, t] = carry[t].astype(BF16)
                    out.append(decx_ref[t, pl.ds(k, 1), :] * carry[t] + in_ref[k, t].astype(F32))
                carry = tuple(out)
            return carry

        lax.fori_loop(0, n // width, lap, tuple(jnp.zeros((16, 128), F32) for _ in range(m)))

    scan_blocks(ercv_ref, ssnd_ref, lambda k: k)
    srcv_ref[me] = ssnd_ref[me]
    copy_s = functools.partial(to_peer, lambda peer: ssnd_ref.at[peer], srcv_ref, sss, rss)
    each_peer(lambda i: copy_s(i).start())

    lax.fori_loop(1, 2, local_pair, 0)

    settle(frcv_ref, ssf, rsf)
    scan_blocks(frcv_ref, gsnd_ref, lambda k: n - 1 - k)
    grcv_ref[me] = gsnd_ref[me]
    copy_g = functools.partial(to_peer, lambda peer: gsnd_ref.at[peer], grcv_ref, ssg, rsg)
    each_peer(lambda i: copy_g(i).start())

    lax.fori_loop(2, PAIRS, local_pair, 0)

    settle(srcv_ref, sss, rss)
    from_slices(srcv_ref, s_ref)

    def s_pair(i, _):
        ds = []
        for k in range(2):
            c = i * 2 + k
            rows = pair_rows(i, k)
            advance(s_ref, e_ref, c, sp_ref)
            gt, sp = gt_ref[rows, :], sp_ref[c]
            out = dot(cz_ref[rows, :], sp)
            ds.append(dot((gt.astype(F32) * out).astype(BF16), fold_in) * mask4)
        hi, lo = split(jnp.concatenate(ds, axis=0))
        sums = dot(hi, suffix, TN) + dot(lo, suffix, TN)
        lg_ref[:, pair_lanes(i)] = lg_ref[:, pair_lanes(i)] + sums[0:GH]
        return 0

    each_pair(s_pair)

    theirs = pl.ds(pl.multiple_of(other * 128, 128), 128)
    mine = pl.ds(pl.multiple_of(core * 128, 128), 128)

    swap = pltpu.make_async_remote_copy(
        src_ref=tsnd_ref, dst_ref=trcv_ref, send_sem=st4, recv_sem=rt4, device_id=(me, other), device_id_type=MESH
    )

    settle(grcv_ref, ssg, rsg)
    from_slices(grcv_ref, g2_ref)

    def g_cross(lap, _):
        i = PAIRS - 1 - lap
        ds = [None, None]
        for k in (1, 0):
            c = i * 2 + k
            rows = pair_rows(i, k)
            advance(g2_ref, f_ref, c, gp_ref)
            gp = gp_ref[c]
            through = sp_ref[c].astype(F32) * gp.astype(F32)
            for g in range(GROUPS):
                part = jnp.sum(through[DIM * g : DIM * g + DIM], axis=0, keepdims=True)
                th_ref[pl.ds(c * GROUPS + g, 1), :] = part
            back = dot(bz_ref[rows, :], gp)
            ds[k] = dot((xt_ref[rows, :].astype(F32) * back).astype(BF16), fold_in) * mask4
            e_ref[c] = back
        hi, lo = split(jnp.concatenate(ds, axis=0))
        sums = dot(hi, before_plain, TN) + dot(lo, before_plain, TN)
        lg_ref[:, pair_lanes(i)] = lg_ref[:, pair_lanes(i)] + sums[0:GH, 0:128]
        al_ref[:, pair_lanes(i)] = al_ref[:, pair_lanes(i)] + sums[0:GH, 128:256]
        return 0

    each_pair(g_cross)

    by_channel = ones(over(iota((WIDE, GH), 0), DIM) == within(iota((WIDE, GH), 1), HEADS), BF16)
    th = add_thirds(dot(thirds(th_ref[...]), by_channel))
    th = jnp.where(within(iota((32, GH), 0), GROUPS) == over(iota((32, GH), 1), HEADS), th, 0.0)
    spread_th = ones(over(iota((96, TOK), 0) & 31, GROUPS) == over(iota((96, TOK), 1), CHUNK), BF16)
    log_grad = lg_ref[...] + dot(thirds(th), spread_th, TN)
    late_rates = jnp.exp(column(alog_ref))
    late_u = dt_ref[...] + column(bias_ref)
    sig = 1.0 / (1.0 + jnp.exp(-late_u))
    graw = (al_ref[...] / step_ref[...] - late_rates * log_grad) * sig
    graw_ref[...] = graw
    alog_col = jnp.sum(log_grad * ld_ref[...], axis=1, keepdims=True)
    bias_col = jnp.sum(graw, axis=1, keepdims=True)
    pick = iota((GH, 128), 0) == iota((GH, 128), 1)
    alog_row = jnp.sum(jnp.where(pick, alog_col, 0.0), axis=0, keepdims=True)
    bias_row = jnp.sum(jnp.where(pick, bias_col, 0.0), axis=0, keepdims=True)
    tail_ref[...] = alog_row + pltpu.roll(bias_row, GH, 1)
    tailall_ref[me] = tail_ref[...]
    tail_copy = functools.partial(to_peer, lambda peer: tail_ref, tailall_ref, ss3, rs3)
    each_peer(lambda i: tail_copy(i).start())

    def bc_pair(i, _):
        gbs, gcs = [], []
        for k in range(2):
            c = i * 2 + k
            rows = pair_rows(i, k)
            gbs.append((wb_ref[c].astype(F32) + dot(gp_ref[c], xt_ref[rows, :], NT) * gmask).astype(BF16))
            gcs.append((wc_ref[c].astype(F32) + dot(sp_ref[c], gt_ref[rows, :], NT) * gmask).astype(BF16))
        gbacc_ref[:, pair_lanes(i)] = dot(jnp.concatenate(gbs, axis=1), r2t_ref[...])
        gcacc_ref[:, pair_lanes(i)] = dot(jnp.concatenate(gcs, axis=1), r2t_ref[...])
        return 0

    twice(bc_pair)
    tsnd_ref[0] = gbacc_ref[theirs, :].astype(BF16)
    tsnd_ref[1] = gcacc_ref[theirs, :].astype(BF16)
    swap.start()

    def gin_pair(i, _):
        for k in range(2):
            rows = pair_rows(i, k)
            gin = (sx_ref[rows, :] * (z_ref[rows, :] + e_ref[i * 2 + k])).astype(BF16)
            gin_ref[tokens_of(i, k)] = gin.reshape(CHUNK, GROUPS, WIDE)
        return 0

    lax.fori_loop(0, PAIRS, gin_pair, 0)
    swap.wait()
    gb_ref[...] = (gbacc_ref[mine, :] + trcv_ref[0].astype(F32)).astype(BF16)
    gc_ref[...] = (gcacc_ref[mine, :] + trcv_ref[1].astype(F32)).astype(BF16)

    settle(tailall_ref, ss3, rs3)
    sums = jnp.sum(tailall_ref[...].reshape(n, 128), axis=0, keepdims=True)
    sums = jnp.where(over(iota((8, 128), 1), HEADS) == iota((8, 128), 0), sums, 0.0)
    ends = add_thirds(dot(thirds(sums), ones(within(iota((128, HEADS), 0), HEADS) == iota((128, HEADS), 1), BF16)))
    galog_ref[...] = ends[0:4]
    gbias_ref[...] = ends[4:8]


def hand_over(*refs):
    ins, outs, sems = refs[:6], refs[6:12], refs[12]
    pairs = [(ins[0].at[pl.ds(128 * i, 128)], outs[0].at[pl.ds(128 * i, 128)]) for i in range(PAIRS)]
    pairs += list(zip(ins[1:], outs[1:]))
    copies = [pltpu.make_async_copy(a, b, sems.at[j]) for j, (a, b) in enumerate(pairs)]
    for copy in copies:
        copy.start()
    for copy in copies:
        copy.wait()


def scratch(n):
    m = TILES // n
    dma = pltpu.SemaphoreType.DMA
    vm = pltpu.VMEM
    slices = (n, m, 16, 128)
    return [
        vm((TOK, GROUPS, WIDE), BF16), vm((TOK, GROUPS, WIDE), BF16),
        vm((GH, TOK), F32), vm((GROUPS, HEADS), F32), vm((GROUPS, HEADS), F32), vm((256, TOK), BF16), vm((256, TOK), BF16),
        vm((TOK, 128), BF16), vm((2048, 128), BF16), vm((2048, WIDE), F32), vm((2048, WIDE), BF16), vm((2048, WIDE), BF16),
        vm((CHUNKS, 256, 256), BF16), vm((CHUNKS, 256, 256), BF16), vm((2048, 256), BF16), vm((2048, 256), BF16),
        vm((CHUNKS, 256, WIDE), F32), vm((CHUNKS, 256, WIDE), F32), vm((32, WIDE), F32),
        vm((256, WIDE), F32), vm((256, WIDE), F32), vm((CHUNKS, 256, WIDE), BF16), vm((CHUNKS, 256, WIDE), BF16),
        vm((2048, WIDE), F32), vm((CHUNKS, 256, 256), BF16), vm((CHUNKS, 256, 256), BF16),
        vm((GH, TOK), F32), vm((GH, TOK), F32), vm((256, TOK), F32), vm((256, TOK), F32),
        vm((32, WIDE), F32), vm((GH, TOK), F32), vm((GH, TOK), F32),
        vm((128, 512), BF16), vm((512, 128), BF16), vm((ROWS, ROWS), F32), vm((ROWS, ROWS), F32), vm((ROWS, ROWS), F32),
        vm((1, 128), F32), vm((n, 1, 128), F32), vm((m, n, 128), F32),
        vm(slices, BF16), vm(slices, BF16), vm(slices, BF16), vm(slices, BF16),
        vm(slices, BF16), vm(slices, BF16), vm(slices, BF16), vm(slices, BF16),
        vm((2, 128, TOK), BF16), vm((2, 128, TOK), BF16), vm((1, 128), F32), vm((n, 1, 128), F32),
        dma, dma, dma, dma, dma, dma, dma, dma, dma, dma, dma, dma, dma, dma, dma((7,)),
    ]


def solution(mesh):
    n = mesh.shape["ctx"]

    def body(inputs, grad_out, dt_raw, dt_bias, a_log, b_proj, c_proj):
        bt = jnp.transpose(b_proj, (1, 2, 0)).reshape(GROUPS * DIM, TOK)
        ct = jnp.transpose(c_proj, (1, 2, 0)).reshape(GROUPS * DIM, TOK)
        vmem = pl.BlockSpec(memory_space=pltpu.VMEM)
        hbm = pl.BlockSpec(memory_space=pl.ANY)
        shapes = [
            jax.ShapeDtypeStruct((TOK, GROUPS, WIDE), BF16),
            jax.ShapeDtypeStruct((GH, TOK), F32),
            jax.ShapeDtypeStruct((GROUPS, HEADS), F32),
            jax.ShapeDtypeStruct((GROUPS, HEADS), F32),
            jax.ShapeDtypeStruct((128, TOK), BF16),
            jax.ShapeDtypeStruct((128, TOK), BF16),
        ]
        results = pl.pallas_call(
            functools.partial(kernel, n),
            out_shape=[pltpu.VMEM(shape.shape, shape.dtype) for shape in shapes],
            in_specs=[hbm] * 7,
            out_specs=[vmem] * 6,
            scratch_shapes=scratch(n),
            compiler_params=pltpu.CompilerParams(
                collective_id=0, has_side_effects=True, vmem_limit_bytes=56 * 2**20
            ),
        )(inputs, grad_out, dt_raw.reshape(GH, TOK), dt_bias, a_log, bt, ct)
        gin, graw, galog, gbias, gb, gc = pl.pallas_call(
            hand_over,
            out_shape=shapes,
            in_specs=[vmem] * 6,
            out_specs=[hbm] * 6,
            scratch_shapes=[pltpu.SemaphoreType.DMA((PAIRS + 5,))],
            compiler_params=pltpu.CompilerParams(vmem_limit_bytes=4 * 2**20),
        )(*results)
        graw = graw.reshape(GROUPS, HEADS, TOK)
        gb = jnp.transpose(gb.reshape(2, DIM, TOK), (2, 0, 1))
        gc = jnp.transpose(gc.reshape(2, DIM, TOK), (2, 0, 1))
        return gin, graw, galog, gbias, gb, gc

    in_specs = (
        P("ctx", None, "tp"),
        P("ctx", None, "tp"),
        P(None, "tp", "ctx"),
        P(None, "tp"),
        P(None, "tp"),
        P("ctx", None, None),
        P("ctx", None, None),
    )
    out_specs = (
        P("ctx", None, "tp"),
        P(None, "tp", "ctx"),
        P(None, "tp"),
        P(None, "tp"),
        P("ctx", "tp", None),
        P("ctx", "tp", None),
    )
    return jax.shard_map(body, mesh=mesh, in_specs=in_specs, out_specs=out_specs, check_vma=False)
```
